512 devices in a mesh: seq: 32 (over x, z_lo), exp: 16 (over z_hi, y, core).
Axes of the slice: x: 4, y: 4, z: 16 (z_hi: 2, z_lo: 8; z = z_hi * 8 + z_lo), core: 2. Of those that a mesh axis runs over, the one named last changes fastest.
Arguments:
- tokens: bfloat16 [8, 8192, 2048], P(None, 'seq', 'exp'), may hold values from -6 to 6
- grad_out: bfloat16 [8, 8192, 2048], P(None, 'seq', 'exp'), may hold values from -6 to 6
- logits: float32 [8, 16, 8192], P(None, None, 'seq'), may hold values from -12 to 312
- slot_params: bfloat16 [16, 2048], P(None, 'exp'), may hold values from -6 to 6
- weight_in: bfloat16 [16, 2048, 4096], P('exp', None, 'seq'), may hold values from -0.125 to 0.125
- weight_out: bfloat16 [16, 4096, 2048], P('exp', 'seq'), may hold values from -0.09375 to 0.09375
Outputs:
- grad_tokens: bfloat16 [8, 8192, 2048], P(None, 'seq', 'exp')
- grad_slots: float32 [16, 2048], P(None, 'exp')
- grad_weight_in: bfloat16 [16, 2048, 4096], P('exp', None, 'seq')
- grad_weight_out: bfloat16 [16, 4096, 2048], P('exp', 'seq')
The draws below stay inside these ranges and needn't reach their ends.
All inputs are finite; a program needn't handle non-finite values.
Results may differ from the reference program's by a relative error of at most 0.024.
Values may be sent and summed in bfloat16 or wider, within the bound.
A program may use at most 64 MiB of HBM per device.

```python
from functools import partial
import jax
import jax.numpy as jnp
from jax import lax

D = 2048
FF = 4096
CLIPS = 8
EXPERTS = 16
TOKENS = 8192


def draw_logits(key, part):
    key = jax.random.fold_in(key, 7)
    base_key = jax.random.fold_in(key, 0)
    shape = (CLIPS, EXPERTS, TOKENS)
    values = 2.5 * jnp.clip(jax.random.normal(base_key, shape, jnp.float32), -4.5, 4.5)
    return values


def steps_of(stream_key, extent, cuts, low, largest):
    level, own = 1.0, jax.random.fold_in(stream_key, 6)
    for axis_at, shards_of in cuts:
        heights = jnp.exp(jax.random.uniform(jax.random.fold_in(own, axis_at), (shards_of,), jnp.float32, low / len(cuts), largest / len(cuts)))
        level = level * jnp.repeat(heights, extent[axis_at] // shards_of).reshape([-1 if axis == axis_at else 1 for axis in range(len(extent))])
    return level


def scatter_about(stream_key, dims, scale, most, shards=(), held_as=jnp.bfloat16):
    level = steps_of(stream_key, dims, shards, -0.22, 0.18) if shards else 1.0
    values = jax.random.normal(stream_key, dims, jnp.float32) * scale * level
    return jnp.minimum(jnp.maximum(values, -most), most).astype(held_as)


def setup_inputs(seed: int = 0) -> dict:
    key_list = jax.random.split(jax.random.key(seed), 7)
    tokens = scatter_about(key_list[0], (CLIPS, TOKENS, D), 1.0, 6.0, ((1, 32), (2, 16)))
    grad_out = scatter_about(key_list[1], (CLIPS, TOKENS, D), 1.0, 6.0, ((1, 32), (2, 16)))
    logits = draw_logits(jax.random.fold_in(key_list[6], 71), 0)
    slot_params = scatter_about(key_list[3], (EXPERTS, D), 1.0, 6.0, ((1, 16),))
    weight_in = scatter_about(key_list[4], (EXPERTS, D, FF), D ** -0.5, 0.125, ((0, 16), (2, 32)))
    weight_out = scatter_about(key_list[5], (EXPERTS, FF, D), FF ** -0.5, 0.09375, ((0, 16), (1, 32)))
    return dict(tokens=tokens, grad_out=grad_out, logits=logits, slot_params=slot_params, weight_in=weight_in, weight_out=weight_out)


root_coef = 0.7978845608028654
cubic_coef = 0.044715


def gelu_parts(pre_act):
    tanh_value = jnp.tanh(root_coef * (pre_act + cubic_coef * pre_act * pre_act * pre_act))
    activated = 0.5 * pre_act * (1.0 + tanh_value)
    derivative = 0.5 * (1.0 + tanh_value) + 0.5 * pre_act * (1.0 - tanh_value * tanh_value) * root_coef * (1.0 + 3.0 * cubic_coef * pre_act * pre_act)
    return activated, derivative


def slot_sums(operands):
    clip_tokens, clip_grads, clip_logits = operands
    dispatch = jax.nn.softmax(clip_logits, axis=1)
    combine = jax.nn.softmax(clip_logits, axis=0)
    slot_in = jnp.dot(dispatch.astype(jnp.bfloat16), clip_tokens, preferred_element_type=jnp.float32)
    slot_grad = jnp.dot(combine.astype(jnp.bfloat16), clip_grads, preferred_element_type=jnp.float32)
    return slot_in, slot_grad


def expert_pass(operands):
    rows_in, rows_grad, expert_in, expert_out = operands
    pre_act = jnp.dot(rows_in, expert_in, preferred_element_type=jnp.float32)
    activated, derivative = gelu_parts(pre_act)
    act_b = activated.astype(jnp.bfloat16)
    slot_out = jnp.dot(act_b, expert_out, preferred_element_type=jnp.float32)
    act_grad = jnp.dot(rows_grad, expert_out.T, preferred_element_type=jnp.float32)
    pre_grad = (act_grad * derivative).astype(jnp.bfloat16)
    grad_out_w = jnp.dot(act_b.T, rows_grad, preferred_element_type=jnp.float32).astype(jnp.bfloat16)
    grad_in_w = jnp.dot(rows_in.T, pre_grad, preferred_element_type=jnp.float32).astype(jnp.bfloat16)
    slot_back = jnp.dot(pre_grad, expert_in.T, preferred_element_type=jnp.float32)
    return slot_out, slot_back, grad_in_w, grad_out_w


def clip_back(slot_params, operands):
    clip_tokens, clip_grads, clip_logits, slot_in, slot_out, slot_back = operands
    dispatch = jax.nn.softmax(clip_logits, axis=1)
    combine = jax.nn.softmax(clip_logits, axis=0)
    out_b = slot_out.astype(jnp.bfloat16)
    back_b = slot_back.astype(jnp.bfloat16)
    comb_grad = jnp.dot(out_b, clip_grads.T, preferred_element_type=jnp.float32)
    disp_grad = jnp.dot(back_b, clip_tokens.T, preferred_element_type=jnp.float32)
    disp_stat = jnp.sum(back_b.astype(jnp.float32) * slot_in, axis=1, keepdims=True)
    logit_grad = combine * (comb_grad - jnp.sum(combine * comb_grad, axis=0, keepdims=True)) + dispatch * (disp_grad - disp_stat)
    token_grad = jnp.dot(dispatch.T, slot_back, precision=lax.Precision.HIGHEST) + jnp.dot(logit_grad.T, slot_params.astype(jnp.float32), precision=lax.Precision.HIGHEST)
    slot_term = jnp.dot(logit_grad.astype(jnp.bfloat16), clip_tokens, preferred_element_type=jnp.float32)
    return token_grad.astype(jnp.bfloat16), slot_term


def reference(tokens, grad_out, logits, slot_params, weight_in, weight_out):
    slot_in, slot_grad = lax.map(slot_sums, (tokens, grad_out, logits))
    rows_in = jnp.swapaxes(slot_in, 0, 1).astype(jnp.bfloat16)
    rows_grad = jnp.swapaxes(slot_grad, 0, 1).astype(jnp.bfloat16)
    slot_out, slot_back, grad_weight_in, grad_weight_out = lax.map(expert_pass, (rows_in, rows_grad, weight_in, weight_out))
    slot_out = jnp.swapaxes(slot_out, 0, 1)
    slot_back = jnp.swapaxes(slot_back, 0, 1)
    grad_tokens, slot_terms = lax.map(partial(clip_back, slot_params), (tokens, grad_out, logits, slot_in, slot_out, slot_back))
    grad_slots = jnp.sum(slot_terms, axis=0)
    return grad_tokens, grad_slots, grad_weight_in, grad_weight_out
```

```python
import functools

import jax
import jax.numpy as jnp
from jax import lax
from jax.experimental import pallas as pl
from jax.experimental.pallas import tpu as pltpu
from jax.sharding import PartitionSpec as P

root_coef = 0.7978845608028654
cubic_coef = 0.044715
MESH = pl.DeviceIdType.MESH
f32 = jnp.float32
bf16 = jnp.bfloat16
LINE = 8


def gelu_parts(pre_act):
    tanh_value = jnp.tanh(root_coef * (pre_act + cubic_coef * pre_act * pre_act * pre_act))
    activated = 0.5 * pre_act * (1.0 + tanh_value)
    derivative = 0.5 * (1.0 + tanh_value) + 0.5 * pre_act * (
        1.0 - tanh_value * tanh_value
    ) * root_coef * (1.0 + 3.0 * cubic_coef * pre_act * pre_act)
    return (activated, derivative)


def dot(a, b, ca, cb):
    return lax.dot_general(a, b, (((ca,), (cb,)), ((), ())), preferred_element_type=f32)


def wait_for(ref, sem):
    pltpu.make_async_copy(ref, ref, sem).wait()


def each(count, step):
    def run(i, carry):
        step(i)
        return carry

    lax.fori_loop(0, count, run, 0)


def kernel(
    S, E, C,
    tokens_h, grad_h, logits_h, params_h, win_h, wout_h,
    gtok_h, gslot_h, gwin_h, gwout_h,
    tokens, grad, logits, params, win, wout,
    gtok, gslot, gwin, gwout,
    comb, disp,
    send1, recv1, send2, rows, send3, recv3, send4, recv4,
    send5, recv5, send6, recv6, recv7, recv8,
    slot_keep, lse_keep,
    in_sem, out_sem, send_sem, recv_sem,
):
    s = lax.axis_index("seq")
    x = lax.axis_index("exp")
    half = LINE // 2
    Q = E // 2
    per = C // Q
    q = lax.rem(x, Q)
    side = x - q
    across = lax.rem(x + Q, E)

    def owner(e):
        return lax.div(e, half) * LINE + LINE // 4 + lax.rem(e, half)

    z = lax.rem(s, LINE)
    is_owner = jnp.logical_and(z >= LINE // 4, z < LINE // 4 + half)
    mine = lax.div(s, LINE) * half + jnp.clip(z - LINE // 4, 0, half - 1)
    both = jnp.logical_and(is_owner, mine == x)
    home = owner(x)

    loads = []
    for i, (a, b) in enumerate(
        ((logits_h, logits), (tokens_h, tokens), (grad_h, grad), (win_h, win), (wout_h, wout), (params_h, params))
    ):
        copy = pltpu.make_async_copy(a, b, in_sem.at[i])
        copy.start()
        loads.append(copy)

    barrier = pltpu.get_barrier_semaphore()

    def greet(ds, dx):
        pl.semaphore_signal(barrier, inc=1, device_id=(ds, dx), device_id_type=MESH)

    each(S - 1, lambda i: greet(lax.rem(s + 1 + i, S), x))
    each(Q - 1, lambda i: greet(s, side + lax.rem(q + 1 + i, Q)))
    greet(s, across)
    each(E - 1, lambda i: greet(home, lax.rem(x + 1 + i, E)))

    @pl.when(jnp.logical_not(both))
    def _():
        greet(home, x)

    @pl.when(is_owner)
    def _():
        each(S - 1, lambda i: greet(lax.rem(s + 1 + i, S), mine))

        @pl.when(jnp.logical_not(both))
        def _():
            greet(s, mine)

    def send(src, dst, k, ds, dx):
        pltpu.make_async_remote_copy(
            src_ref=src, dst_ref=dst, send_sem=send_sem.at[k], recv_sem=recv_sem.at[k],
            device_id=(ds, dx), device_id_type=MESH,
        ).start()

    def keep(src, dst, k):
        pltpu.make_async_copy(src, dst, recv_sem.at[k]).start()

    def sent(ref, k):
        wait_for(ref, send_sem.at[k])

    loads[0].wait()
    loads[1].wait()
    loads[2].wait()
    slot_parts, grad_parts, lse_parts = [], [], []
    for c in range(C):
        value = logits[c]
        top = jnp.max(value, axis=1, keepdims=True)
        weight = jnp.exp(value - top)
        mass = jnp.sum(weight, axis=1, keepdims=True)
        slot_parts.append(dot((weight / mass).astype(bf16), tokens[c], 1, 0))
        lse_parts.append(jnp.broadcast_to(top + jnp.log(mass), (E, 128)))
        crest = jnp.max(value, axis=0, keepdims=True)
        share = jnp.exp(value - crest)
        share = share / jnp.sum(share, axis=0, keepdims=True)
        comb[c] = share
        grad_parts.append(dot(share.astype(bf16), grad[c], 1, 0))
    send1[:, 0:8, :] = jnp.swapaxes(jnp.stack(slot_parts), 0, 1)
    send1[:, 8:16, :] = jnp.swapaxes(jnp.stack(grad_parts), 0, 1)
    send1[:, 16:24, :] = jnp.swapaxes(jnp.stack(lse_parts), 0, 1)

    flag = is_owner.astype(jnp.int32)
    pl.semaphore_wait(barrier, S - 1 + Q - 1 + 1 + E + flag * S - 2 * both.astype(jnp.int32))

    def to_owner(i):
        e = lax.rem(x + s + i, E)
        to = owner(e)

        @pl.when(to != s)
        def _():
            send(send1.at[e], recv1.at[s], 0, to, x)

        @pl.when(to == s)
        def _():
            keep(send1.at[e], recv1.at[s], 0)

    each(E, to_owner)

    @pl.when(is_owner)
    def _():
        wait_for(recv1, recv_sem.at[0])
        top = lax.fori_loop(1, S, lambda i, t: jnp.maximum(t, recv1[i, 16:24, :]), recv1[0, 16:24, :])

        def add(i, carry):
            total, slots, grads = carry
            weight = jnp.exp(recv1[i, 16:24, :] - top)
            return total + weight, slots + weight * recv1[i, 0:8, :], grads + recv1[i, 8:16, :]

        zero = jnp.zeros((8, 128), f32)
        total, slots, grads = lax.fori_loop(0, S, add, (zero, zero, zero))
        slots = slots / total
        slot_keep[...] = slots
        lse_keep[...] = top + jnp.log(total)
        send2[...] = jnp.concatenate([slots, grads], axis=0).astype(bf16)

        each(S - 1, lambda i: send(send2, rows.at[x], 1, lax.rem(s + 1 + i, S), mine))

        @pl.when(jnp.logical_not(both))
        def _():
            send(send2, rows.at[x], 1, s, mine)

        @pl.when(both)
        def _():
            keep(send2, rows.at[x], 1)

    loads[3].wait()
    loads[4].wait()
    wait_for(rows, recv_sem.at[1])
    held = jnp.concatenate([rows[i] for i in range(E)], axis=1)
    pre_act = dot(held, win[...], 1, 0)
    act_grad = dot(held, wout[...], 1, 1)
    activated, derivative = gelu_parts(pre_act[0:8])
    pre_grad = act_grad[8:16] * derivative
    stacked = jnp.concatenate([activated, pre_grad], axis=0).astype(bf16)
    out_part = dot(stacked, wout[...], 1, 0)
    back_part = dot(stacked, win[...], 1, 1)
    for i in range(E):
        cut = slice(i * 128, i * 128 + 128)
        send3[i] = jnp.concatenate([out_part[0:8, cut], back_part[8:16, cut]], axis=0).astype(bf16)

    def to_home(i):
        to = lax.rem(x + s + i, E)
        own = jnp.logical_and(both, to == x)

        @pl.when(jnp.logical_not(own))
        def _():
            send(send3.at[to], recv3.at[s], 2, home, to)

        @pl.when(own)
        def _():
            keep(send3.at[to], recv3.at[s], 2)

    each(E, to_home)

    blank = jnp.zeros((8, 128), f32)
    gwout[...] = dot(jnp.concatenate([blank, activated], axis=0).astype(bf16), held, 0, 0).astype(bf16)
    gwin[...] = dot(held, jnp.concatenate([pre_grad, blank], axis=0).astype(bf16), 0, 0).astype(bf16)
    store_out = pltpu.make_async_copy(gwout, gwout_h, out_sem.at[0])
    store_in = pltpu.make_async_copy(gwin, gwin_h, out_sem.at[1])
    store_out.start()
    store_in.start()

    @pl.when(is_owner)
    def _():
        wait_for(recv3, recv_sem.at[2])
        total = lax.fori_loop(0, S, lambda i, t: t + recv3[i].astype(f32), jnp.zeros((16, 128), f32))
        send4[0:16, :] = total
        stat = jnp.sum(total[8:16].astype(bf16).astype(f32) * slot_keep[...], axis=1, keepdims=True)
        lane = lax.broadcasted_iota(jnp.int32, (8, 128), 1)
        send4[16:24, :] = jnp.where(lane < 64, lse_keep[...], stat)
        each(S - 1, lambda i: send(send4, recv4.at[mine], 3, lax.rem(s + 1 + i, S), x))
        keep(send4, recv4.at[mine], 3)

    wait_for(recv4, recv_sem.at[3])
    outs = jnp.swapaxes(recv4[:, 0:8, :], 0, 1)
    backs = jnp.swapaxes(recv4[:, 8:16, :], 0, 1)
    stats = jnp.swapaxes(recv4[:, 16:24, :], 0, 1)
    for c in range(C):
        comb_grad = dot(outs[c].astype(bf16), grad[c], 1, 1)
        disp_grad = dot(backs[c].astype(bf16), tokens[c], 1, 1)
        dispatch = jnp.exp(logits[c] - stats[c][:, 0:1])
        share = comb[c]
        disp[c] = dispatch
        send5[c] = share * (
            comb_grad - jnp.sum(share * comb_grad, axis=0, keepdims=True)
        ) + dispatch * (disp_grad - stats[c][:, 64:65])

    def to_peer(i):
        to = lax.rem(q + 1 + i, Q)
        send(send5.at[pl.ds(to * per, per)], recv5.at[q], 4, s, side + to)

    each(Q - 1, to_peer)
    keep(send5.at[pl.ds(q * per, per)], recv5.at[q], 4)
    wait_for(recv5, recv_sem.at[4])
    part = recv5[0]
    for i in range(1, Q):
        part = part + recv5[i]
    send6[...] = part
    send(send6, recv6, 5, s, across)
    wait_for(recv6, recv_sem.at[5])
    recv7[q] = (send6[...] + recv6[...]).astype(bf16)
    each(Q - 1, lambda i: send(recv7.at[q], recv7.at[q], 6, s, side + lax.rem(q + 1 + i, Q)))
    loads[5].wait()
    wait_for(recv7.at[pl.ds(0, Q - 1)], recv_sem.at[6])

    term = jnp.zeros((E, 128), f32)
    for c in range(C):
        term = term + dot(recv7[c // per, c % per], tokens[c], 1, 0)
    recv8[s] = term.astype(bf16)
    each(S - 1, lambda i: send(recv8.at[s], recv8.at[s], 7, lax.rem(s + 1 + i, S), x))

    for c in range(C):
        left = jnp.concatenate([disp[c].astype(bf16), recv7[c // per, c % per]], axis=0)
        right = jnp.concatenate([backs[c].astype(bf16), params[...]], axis=0)
        gtok[c] = dot(left, right, 0, 0).astype(bf16)
    store_tok = pltpu.make_async_copy(gtok, gtok_h, out_sem.at[2])
    store_tok.start()

    wait_for(recv8.at[pl.ds(0, S - 1)], recv_sem.at[7])
    total = recv8[0].astype(f32)
    for i in range(1, S):
        total = total + recv8[i].astype(f32)
    gslot[...] = total
    store_slot = pltpu.make_async_copy(gslot, gslot_h, out_sem.at[3])
    store_slot.start()

    sent(send1.at[pl.ds(0, E - 1)], 0)

    @pl.when(jnp.logical_not(is_owner))
    def _():
        sent(send1.at[0], 0)

    @pl.when(is_owner)
    def _():
        each(S - 1, lambda i: sent(send2, 1))

        @pl.when(jnp.logical_not(both))
        def _():
            sent(send2, 1)

        each(S - 1, lambda i: sent(send4, 3))

    sent(send3.at[pl.ds(0, E - 1)], 2)

    @pl.when(jnp.logical_not(both))
    def _():
        sent(send3.at[0], 2)

    sent(recv5.at[pl.ds(0, Q - 1)], 4)
    sent(send6, 5)
    sent(recv7.at[pl.ds(0, Q - 1)], 6)
    sent(recv8.at[pl.ds(0, S - 1)], 7)
    store_out.wait()
    store_in.wait()
    store_tok.wait()
    store_slot.wait()


def solution(mesh):
    S, E = mesh.shape["seq"], mesh.shape["exp"]

    def body(tokens, grad_out, logits, slot_params, weight_in, weight_out):
        C, M, D = tokens.shape
        _, wide, F = weight_in.shape
        args = (tokens, grad_out, logits, slot_params, weight_in[0], weight_out[0])
        outs = (
            jax.ShapeDtypeStruct((C, M, D), bf16),
            jax.ShapeDtypeStruct((E, D), f32),
            jax.ShapeDtypeStruct((wide, F), bf16),
            jax.ShapeDtypeStruct((F, wide), bf16),
        )
        Q = E // 2
        per = C // Q
        hold = lambda a: pltpu.VMEM(a.shape, a.dtype)
        scratch = (
            [hold(a) for a in args]
            + [hold(a) for a in outs]
            + [
                pltpu.VMEM((C, E, M), f32),
                pltpu.VMEM((C, E, M), f32),
                pltpu.VMEM((E, 24, D), f32),
                pltpu.VMEM((S, 24, D), f32),
                pltpu.VMEM((16, D), bf16),
                pltpu.VMEM((E, 16, D), bf16),
                pltpu.VMEM((E, 16, D), bf16),
                pltpu.VMEM((S, 16, D), bf16),
                pltpu.VMEM((24, D), f32),
                pltpu.VMEM((E, 24, D), f32),
                pltpu.VMEM((C, E, M), f32),
                pltpu.VMEM((Q, per, E, M), f32),
                pltpu.VMEM((per, E, M), f32),
                pltpu.VMEM((per, E, M), f32),
                pltpu.VMEM((Q, per, E, M), bf16),
                pltpu.VMEM((S, E, D), bf16),
                pltpu.VMEM((8, D), f32),
                pltpu.VMEM((8, D), f32),
                pltpu.SemaphoreType.DMA((6,)),
                pltpu.SemaphoreType.DMA((4,)),
                pltpu.SemaphoreType.DMA((8,)),
                pltpu.SemaphoreType.DMA((8,)),
            ]
        )
        gtok, gslot, gwin, gwout = pl.pallas_call(
            functools.partial(kernel, S, E, C),
            out_shape=outs,
            in_specs=[pl.BlockSpec(memory_space=pl.ANY)] * 6,
            out_specs=[pl.BlockSpec(memory_space=pl.ANY)] * 4,
            scratch_shapes=scratch,
            compiler_params=pltpu.CompilerParams(
                collective_id=0, has_side_effects=True, vmem_limit_bytes=48 << 20
            ),
            name="moe_backward",
        )(*args)
        return gtok, gslot, gwin[None], gwout[None]

    in_specs = (
        P(None, "seq", "exp"),
        P(None, "seq", "exp"),
        P(None, None, "seq"),
        P(None, "exp"),
        P("exp", None, "seq"),
        P("exp", "seq", None),
    )
    out_specs = (
        P(None, "seq", "exp"),
        P(None, "exp"),
        P("exp", None, "seq"),
        P("exp", "seq", None),
    )
    return jax.shard_map(body, mesh=mesh, in_specs=in_specs, out_specs=out_specs, check_vma=False)
```

```python
import functools

import jax
import jax.numpy as jnp
from jax import lax
from jax.experimental import pallas as pl
from jax.experimental.pallas import tpu as pltpu
from jax.sharding import PartitionSpec as P

root_coef = 0.7978845608028654
cubic_coef = 0.044715
MESH = pl.DeviceIdType.MESH
f32 = jnp.float32
bf16 = jnp.bfloat16
LINE = 8


def gelu_parts(pre_act):
    tanh_value = jnp.tanh(root_coef * (pre_act + cubic_coef * pre_act * pre_act * pre_act))
    activated = 0.5 * pre_act * (1.0 + tanh_value)
    derivative = 0.5 * (1.0 + tanh_value) + 0.5 * pre_act * (
        1.0 - tanh_value * tanh_value
    ) * root_coef * (1.0 + 3.0 * cubic_coef * pre_act * pre_act)
    return (activated, derivative)


def dot(a, b, ca, cb):
    return lax.dot_general(a, b, (((ca,), (cb,)), ((), ())), preferred_element_type=f32)


def wait_for(ref, sem):
    pltpu.make_async_copy(ref, ref, sem).wait()


def each(count, step):
    def run(i, carry):
        step(i)
        return carry

    lax.fori_loop(0, count, run, 0)


def kernel(
    S, E, C,
    tokens_h, grad_h, logits_h, params_h, win_h, wout_h,
    gtok_h, gslot_h, gwin_h, gwout_h,
    tokens, grad, logits, params, win, wout,
    gtok, gslot, gwin, gwout,
    comb, disp,
    send1, recv1, send2, rows, send3, recv3, send4, recv4,
    row1, rows1, row4, rows4, turned,
    send5, recv5, send6, recv6, recv7, recv8,
    slot_keep, lse_keep,
    in_sem, out_sem, send_sem, recv_sem,
):
    s = lax.axis_index("seq")
    x = lax.axis_index("exp")
    half = LINE // 2
    Q = E // 2
    per = C // Q
    q = lax.rem(x, Q)
    side = x - q
    across = lax.rem(x + Q, E)

    def owner(e):
        return lax.div(e, half) * LINE + LINE // 4 + lax.rem(e, half)

    z = lax.rem(s, LINE)
    is_owner = jnp.logical_and(z >= LINE // 4, z < LINE // 4 + half)
    mine = lax.div(s, LINE) * half + jnp.clip(z - LINE // 4, 0, half - 1)
    both = jnp.logical_and(is_owner, mine == x)
    home = owner(x)

    loads = []
    for i, (a, b) in enumerate(
        ((logits_h, logits), (tokens_h, tokens), (grad_h, grad), (win_h, win), (wout_h, wout), (params_h, params))
    ):
        copy = pltpu.make_async_copy(a, b, in_sem.at[i])
        copy.start()
        loads.append(copy)

    barrier = pltpu.get_barrier_semaphore()

    def greet(ds, dx):
        pl.semaphore_signal(barrier, inc=1, device_id=(ds, dx), device_id_type=MESH)

    each(S - 1, lambda i: greet(lax.rem(s + 1 + i, S), x))
    each(Q - 1, lambda i: greet(s, side + lax.rem(q + 1 + i, Q)))
    greet(s, across)
    each(E - 1, lambda i: greet(home, lax.rem(x + 1 + i, E)))

    @pl.when(jnp.logical_not(both))
    def _():
        greet(home, x)

    @pl.when(is_owner)
    def _():
        each(S - 1, lambda i: greet(lax.rem(s + 1 + i, S), mine))

        @pl.when(jnp.logical_not(both))
        def _():
            greet(s, mine)

    def send(src, dst, k, ds, dx):
        pltpu.make_async_remote_copy(
            src_ref=src, dst_ref=dst, send_sem=send_sem.at[k], recv_sem=recv_sem.at[k],
            device_id=(ds, dx), device_id_type=MESH,
        ).start()

    def keep(src, dst, k):
        pltpu.make_async_copy(src, dst, recv_sem.at[k]).start()

    pending = []

    def sent(ref, k):
        wait_for(ref, send_sem.at[k])

    def diagonal(count, shift):
        down = lax.broadcasted_iota(jnp.int32, (count, 128), 0)
        along = lax.broadcasted_iota(jnp.int32, (count, 128), 1)
        return along == down + shift

    loads[0].wait()
    loads[1].wait()
    loads[2].wait()
    slot_parts, grad_parts, lse_parts = [], [], []
    for c in range(C):
        value = logits[c]
        top = jnp.max(value, axis=1, keepdims=True)
        weight = jnp.exp(value - top)
        mass = jnp.sum(weight, axis=1, keepdims=True)
        slot_parts.append(dot((weight / mass).astype(bf16), tokens[c], 1, 0))
        lse_parts.append(jnp.broadcast_to(top + jnp.log(mass), (E, 128)))
        crest = jnp.max(value, axis=0, keepdims=True)
        share = jnp.exp(value - crest)
        share = share / jnp.sum(share, axis=0, keepdims=True)
        comb[c] = share
        grad_parts.append(dot(share.astype(bf16), grad[c], 1, 0))
    send1[...] = jnp.concatenate(
        [jnp.swapaxes(jnp.stack(slot_parts), 0, 1), jnp.swapaxes(jnp.stack(grad_parts), 0, 1)], axis=1
    ).astype(bf16)
    spread = jnp.swapaxes(jnp.stack(lse_parts), 0, 1).reshape(E * 8, 128)
    row1[...] = jnp.sum(jnp.where(diagonal(E * 8, 0), spread, 0.0), axis=0, keepdims=True)

    flag = is_owner.astype(jnp.int32)
    pl.semaphore_wait(barrier, S - 1 + Q - 1 + 1 + E + flag * S - 2 * both.astype(jnp.int32))

    def to_owner(i):
        e = lax.rem(x + s + i, E)
        to = owner(e)

        @pl.when(to != s)
        def _():
            send(row1, rows1.at[pl.ds(s, 1)], 8, to, x)
            send(send1.at[e], recv1.at[s], 0, to, x)

        @pl.when(to == s)
        def _():
            keep(row1, rows1.at[pl.ds(s, 1)], 8)
            keep(send1.at[e], recv1.at[s], 0)

    each(E, to_owner)

    def sent_first():
        sent(send1.at[pl.ds(0, E - 1)], 0)
        each(E - 1, lambda i: sent(row1, 8))

        @pl.when(jnp.logical_not(is_owner))
        def _():
            sent(send1.at[0], 0)
            sent(row1, 8)

    pending.append(sent_first)

    @pl.when(is_owner)
    def _():
        wait_for(rows1, recv_sem.at[8])
        turned[...] = jnp.transpose(rows1[...])
        lses = turned[pl.ds(pl.multiple_of(mine * 8, 8), 8), :]
        top = jnp.max(lses, axis=1, keepdims=True)
        weights = jnp.exp(lses - top)
        total = jnp.sum(weights, axis=1, keepdims=True)
        weights = weights / total
        lse_keep[...] = jnp.broadcast_to(top + jnp.log(total), (8, 128))
        wait_for(recv1, recv_sem.at[0])
        slots = jnp.zeros((8, 128), f32)
        grads = jnp.zeros((8, 128), f32)
        for i in range(S):
            piece = recv1[i].astype(f32)
            slots = slots + weights[:, i : i + 1] * piece[0:8]
            grads = grads + piece[8:16]
        slot_keep[...] = slots
        send2[...] = jnp.concatenate([slots, grads], axis=0).astype(bf16)

        each(S - 1, lambda i: send(send2, rows.at[x], 1, lax.rem(s + 1 + i, S), mine))

        @pl.when(jnp.logical_not(both))
        def _():
            send(send2, rows.at[x], 1, s, mine)

        @pl.when(both)
        def _():
            keep(send2, rows.at[x], 1)

    def sent_rows():
        @pl.when(is_owner)
        def _():
            each(S - 1, lambda i: sent(send2, 1))

            @pl.when(jnp.logical_not(both))
            def _():
                sent(send2, 1)

    pending.append(sent_rows)
    loads[3].wait()
    loads[4].wait()
    wait_for(rows, recv_sem.at[1])
    held = jnp.concatenate([rows[i] for i in range(E)], axis=1)
    pre_act = dot(held, win[...], 1, 0)
    act_grad = dot(held, wout[...], 1, 1)
    activated, derivative = gelu_parts(pre_act[0:8])
    pre_grad = act_grad[8:16] * derivative
    stacked = jnp.concatenate([activated, pre_grad], axis=0).astype(bf16)
    out_part = dot(stacked, wout[...], 1, 0)
    back_part = dot(stacked, win[...], 1, 1)
    for i in range(E):
        cut = slice(i * 128, i * 128 + 128)
        send3[i] = jnp.concatenate([out_part[0:8, cut], back_part[8:16, cut]], axis=0).astype(bf16)

    def to_home(i):
        to = lax.rem(x + s + i, E)
        own = jnp.logical_and(both, to == x)

        @pl.when(jnp.logical_not(own))
        def _():
            send(send3.at[to], recv3.at[s], 2, home, to)

        @pl.when(own)
        def _():
            keep(send3.at[to], recv3.at[s], 2)

    each(E, to_home)

    def sent_parts():
        sent(send3.at[pl.ds(0, E - 1)], 2)

        @pl.when(jnp.logical_not(both))
        def _():
            sent(send3.at[0], 2)

    pending.append(sent_parts)

    blank = jnp.zeros((8, 128), f32)
    gwout[...] = dot(jnp.concatenate([blank, activated], axis=0).astype(bf16), held, 0, 0).astype(bf16)
    gwin[...] = dot(held, jnp.concatenate([pre_grad, blank], axis=0).astype(bf16), 0, 0).astype(bf16)
    store_out = pltpu.make_async_copy(gwout, gwout_h, out_sem.at[0])
    store_in = pltpu.make_async_copy(gwin, gwin_h, out_sem.at[1])
    store_out.start()
    store_in.start()

    @pl.when(is_owner)
    def _():
        wait_for(recv3, recv_sem.at[2])
        total = lax.fori_loop(0, S, lambda i, t: t + recv3[i].astype(f32), jnp.zeros((16, 128), f32))
        send4[...] = total.astype(bf16)
        stat = jnp.sum(total[8:16].astype(bf16).astype(f32) * slot_keep[...], axis=1, keepdims=True)
        row4[...] = jnp.sum(
            jnp.where(diagonal(8, 0), lse_keep[...], jnp.where(diagonal(8, 8), stat, 0.0)), axis=0, keepdims=True
        )

        def to_line(i):
            to = lax.rem(s + 1 + i, S)
            send(row4, rows4.at[pl.ds(mine, 1)], 9, to, x)
            send(send4, recv4.at[mine], 3, to, x)

        each(S - 1, to_line)
        keep(row4, rows4.at[pl.ds(mine, 1)], 9)
        keep(send4, recv4.at[mine], 3)

    def sent_sums():
        @pl.when(is_owner)
        def _():
            each(S - 1, lambda i: sent(send4, 3))
            each(S - 1, lambda i: sent(row4, 9))

    pending.append(sent_sums)
    wait_for(recv4, recv_sem.at[3])
    wait_for(rows4, recv_sem.at[9])
    sums = recv4[...].astype(f32)
    outs = jnp.swapaxes(sums[:, 0:8, :], 0, 1).astype(bf16)
    backs = jnp.swapaxes(sums[:, 8:16, :], 0, 1).astype(bf16)
    scales = rows4[...]
    for c in range(C):
        comb_grad = dot(outs[c], grad[c], 1, 1)
        disp_grad = dot(backs[c], tokens[c], 1, 1)
        dispatch = jnp.exp(logits[c] - scales[:, c : c + 1])
        share = comb[c]
        disp[c] = dispatch
        send5[c] = share * (
            comb_grad - jnp.sum(share * comb_grad, axis=0, keepdims=True)
        ) + dispatch * (disp_grad - scales[:, C + c : C + c + 1])

    def to_peer(i):
        to = lax.rem(q + 1 + i, Q)
        send(send5.at[pl.ds(to * per, per)], recv5.at[q], 4, s, side + to)

    each(Q - 1, to_peer)
    pending.append(lambda: sent(recv5.at[pl.ds(0, Q - 1)], 4))
    keep(send5.at[pl.ds(q * per, per)], recv5.at[q], 4)
    wait_for(recv5, recv_sem.at[4])
    part = recv5[0]
    for i in range(1, Q):
        part = part + recv5[i]
    send6[...] = part
    send(send6, recv6, 5, s, across)
    pending.append(lambda: sent(send6, 5))
    wait_for(recv6, recv_sem.at[5])
    recv7[q] = (send6[...] + recv6[...]).astype(bf16)
    each(Q - 1, lambda i: send(recv7.at[q], recv7.at[q], 6, s, side + lax.rem(q + 1 + i, Q)))
    pending.append(lambda: sent(recv7.at[pl.ds(0, Q - 1)], 6))
    loads[5].wait()
    wait_for(recv7.at[pl.ds(0, Q - 1)], recv_sem.at[6])

    term = jnp.zeros((E, 128), f32)
    for c in range(C):
        term = term + dot(recv7[c // per, c % per], tokens[c], 1, 0)
    recv8[s] = term.astype(bf16)
    each(S - 1, lambda i: send(recv8.at[s], recv8.at[s], 7, lax.rem(s + 1 + i, S), x))
    pending.append(lambda: sent(recv8.at[pl.ds(0, S - 1)], 7))

    for c in range(C):
        left = jnp.concatenate([disp[c].astype(bf16), recv7[c // per, c % per]], axis=0)
        right = jnp.concatenate([backs[c], params[...]], axis=0)
        gtok[c] = dot(left, right, 0, 0).astype(bf16)
    store_tok = pltpu.make_async_copy(gtok, gtok_h, out_sem.at[2])
    store_tok.start()

    wait_for(recv8.at[pl.ds(0, S - 1)], recv_sem.at[7])
    total = recv8[0].astype(f32)
    for i in range(1, S):
        total = total + recv8[i].astype(f32)
    gslot[...] = total
    store_slot = pltpu.make_async_copy(gslot, gslot_h, out_sem.at[3])
    store_slot.start()

    for wait in pending:
        wait()
    store_out.wait()
    store_in.wait()
    store_tok.wait()
    store_slot.wait()


def hand_over(a, b, c, d, to_a, to_b, to_c, to_d, sem):
    copies = [
        pltpu.make_async_copy(src, dst, sem.at[i])
        for i, (src, dst) in enumerate(((a, to_a), (b, to_b), (c, to_c), (d, to_d)))
    ]
    for copy in copies:
        copy.start()
    for copy in copies:
        copy.wait()


def solution(mesh):
    S, E = mesh.shape["seq"], mesh.shape["exp"]

    def body(tokens, grad_out, logits, slot_params, weight_in, weight_out):
        C, M, D = tokens.shape
        _, wide, F = weight_in.shape
        args = (tokens, grad_out, logits, slot_params, weight_in[0], weight_out[0])
        outs = (
            jax.ShapeDtypeStruct((C, M, D), bf16),
            jax.ShapeDtypeStruct((E, D), f32),
            jax.ShapeDtypeStruct((wide, F), bf16),
            jax.ShapeDtypeStruct((F, wide), bf16),
        )
        Q = E // 2
        per = C // Q
        hold = lambda a: pltpu.VMEM(a.shape, a.dtype)
        scratch = (
            [hold(a) for a in args]
            + [hold(a) for a in outs]
            + [
                pltpu.VMEM((C, E, M), f32),
                pltpu.VMEM((C, E, M), f32),
                pltpu.VMEM((E, 16, D), bf16),
                pltpu.VMEM((S, 16, D), bf16),
                pltpu.VMEM((16, D), bf16),
                pltpu.VMEM((E, 16, D), bf16),
                pltpu.VMEM((E, 16, D), bf16),
                pltpu.VMEM((S, 16, D), bf16),
                pltpu.VMEM((16, D), bf16),
                pltpu.VMEM((E, 16, D), bf16),
                pltpu.VMEM((1, 128), f32),
                pltpu.VMEM((S, 128), f32),
                pltpu.VMEM((1, 128), f32),
                pltpu.VMEM((E, 128), f32),
                pltpu.VMEM((128, S), f32),
                pltpu.VMEM((C, E, M), f32),
                pltpu.VMEM((Q, per, E, M), f32),
                pltpu.VMEM((per, E, M), f32),
                pltpu.VMEM((per, E, M), f32),
                pltpu.VMEM((Q, per, E, M), bf16),
                pltpu.VMEM((S, E, D), bf16),
                pltpu.VMEM((8, D), f32),
                pltpu.VMEM((8, D), f32),
                pltpu.SemaphoreType.DMA((6,)),
                pltpu.SemaphoreType.DMA((4,)),
                pltpu.SemaphoreType.DMA((10,)),
                pltpu.SemaphoreType.DMA((10,)),
            ]
        )
        gtok, gslot, gwin, gwout = pl.pallas_call(
            functools.partial(kernel, S, E, C),
            out_shape=outs,
            in_specs=[pl.BlockSpec(memory_space=pl.ANY)] * 6,
            out_specs=[pl.BlockSpec(memory_space=pl.ANY)] * 4,
            scratch_shapes=scratch,
            compiler_params=pltpu.CompilerParams(
                collective_id=0, has_side_effects=True, vmem_limit_bytes=60 << 20
            ),
            name="moe_backward",
        )(*args)
        gtok, gslot, gwin, gwout = pl.pallas_call(
            hand_over,
            out_shape=outs,
            in_specs=[pl.BlockSpec(memory_space=pl.ANY)] * 4,
            out_specs=[pl.BlockSpec(memory_space=pl.ANY)] * 4,
            scratch_shapes=[pltpu.SemaphoreType.DMA((4,))],
            name="hand_over",
        )(gtok, gslot, gwin, gwout)
        return gtok, gslot, gwin[None], gwout[None]

    in_specs = (
        P(None, "seq", "exp"),
        P(None, "seq", "exp"),
        P(None, None, "seq"),
        P(None, "exp"),
        P("exp", None, "seq"),
        P("exp", "seq", None),
    )
    out_specs = (
        P(None, "seq", "exp"),
        P(None, "exp"),
        P("exp", None, "seq"),
        P("exp", "seq", None),
    )
    return jax.shard_map(body, mesh=mesh, in_specs=in_specs, out_specs=out_specs, check_vma=False)
```

```python
import functools

import jax
import jax.numpy as jnp
from jax import lax
from jax.experimental import pallas as pl
from jax.experimental.pallas import tpu as pltpu
from jax.sharding import PartitionSpec as P

root_coef = 0.7978845608028654
cubic_coef = 0.044715
MESH = pl.DeviceIdType.MESH
f32 = jnp.float32
bf16 = jnp.bfloat16
LINE = 8


def gelu_parts(pre_act):
    tanh_value = jnp.tanh(root_coef * (pre_act + cubic_coef * pre_act * pre_act * pre_act))
    activated = 0.5 * pre_act * (1.0 + tanh_value)
    derivative = 0.5 * (1.0 + tanh_value) + 0.5 * pre_act * (
        1.0 - tanh_value * tanh_value
    ) * root_coef * (1.0 + 3.0 * cubic_coef * pre_act * pre_act)
    return (activated, derivative)


def dot(a, b, ca, cb):
    return lax.dot_general(a, b, (((ca,), (cb,)), ((), ())), preferred_element_type=f32)


def wait_for(ref, sem):
    pltpu.make_async_copy(ref, ref, sem).wait()


def each(count, step):
    def run(i, carry):
        step(i)
        return carry

    lax.fori_loop(0, count, run, 0)


def kernel(
    S, E, C,
    tokens_h, grad_h, logits_h, params_h, win_h, wout_h,
    gtok_h, gslot_h, gwin_h, gwout_h,
    tokens, grad, logits, params, win, wout,
    gtok, gslot, gwin, gwout,
    comb, disp,
    send1, recv1, send2, rows, send3, recv3, send4, recv4,
    row1, rows1, row4, rows4, turned,
    send5, recv5, send6, recv6, recv7, recv8,
    slot_keep, lse_keep,
    in_sem, out_sem, send_sem, recv_sem, go_sem,
):
    s = lax.axis_index("seq")
    x = lax.axis_index("exp")
    half = LINE // 2
    Q = E // 2
    per = C // Q
    q = lax.rem(x, Q)
    side = x - q
    across = lax.rem(x + Q, E)

    def owner(e):
        return lax.div(e, half) * LINE + LINE // 4 + lax.rem(e, half)

    z = lax.rem(s, LINE)
    is_owner = jnp.logical_and(z >= LINE // 4, z < LINE // 4 + half)
    mine = lax.div(s, LINE) * half + jnp.clip(z - LINE // 4, 0, half - 1)
    both = jnp.logical_and(is_owner, mine == x)
    home = owner(x)

    loads = []
    for i, (a, b) in enumerate(
        ((logits_h, logits), (tokens_h, tokens), (grad_h, grad), (win_h, win), (wout_h, wout), (params_h, params))
    ):
        copy = pltpu.make_async_copy(a, b, in_sem.at[i])
        copy.start()
        loads.append(copy)

    barrier = pltpu.get_barrier_semaphore()

    def greet(ds, dx):
        pl.semaphore_signal(barrier, inc=1, device_id=(ds, dx), device_id_type=MESH)

    @pl.when(is_owner)
    def _():
        def to_rest(i):
            k = lax.rem(i + s, S - E)
            zz = lax.rem(k, half)
            greet(lax.div(k, half) * LINE + jnp.where(zz < LINE // 4, zz, zz + half), x)

        each(S - E, to_rest)

    def to_far(i):
        to = lax.rem(x + Q + i, E)

        @pl.when(jnp.logical_or(jnp.logical_not(both), to != x))
        def _():
            greet(home, to)

    each(E, to_far)

    def send(src, dst, k, ds, dx):
        pltpu.make_async_remote_copy(
            src_ref=src, dst_ref=dst, send_sem=send_sem.at[k], recv_sem=recv_sem.at[k],
            device_id=(ds, dx), device_id_type=MESH,
        ).start()

    def keep(src, dst, k):
        pltpu.make_async_copy(src, dst, recv_sem.at[k]).start()

    pending = []

    def sent(ref, k):
        wait_for(ref, send_sem.at[k])

    def diagonal(count, shift):
        down = lax.broadcasted_iota(jnp.int32, (count, 128), 0)
        along = lax.broadcasted_iota(jnp.int32, (count, 128), 1)
        return along == down + shift

    loads[0].wait()
    loads[1].wait()
    loads[2].wait()
    slot_parts, grad_parts, lse_parts = [], [], []
    for c in range(C):
        value = logits[c]
        top = jnp.max(value, axis=1, keepdims=True)
        weight = jnp.exp(value - top)
        mass = jnp.sum(weight, axis=1, keepdims=True)
        slot_parts.append(dot((weight / mass).astype(bf16), tokens[c], 1, 0))
        lse_parts.append(jnp.broadcast_to(top + jnp.log(mass), (E, 128)))
        crest = jnp.max(value, axis=0, keepdims=True)
        share = jnp.exp(value - crest)
        share = share / jnp.sum(share, axis=0, keepdims=True)
        comb[c] = share
        grad_parts.append(dot(share.astype(bf16), grad[c], 1, 0))
    send1[...] = jnp.concatenate(
        [jnp.swapaxes(jnp.stack(slot_parts), 0, 1), jnp.swapaxes(jnp.stack(grad_parts), 0, 1)], axis=1
    ).astype(bf16)
    spread = jnp.swapaxes(jnp.stack(lse_parts), 0, 1).reshape(E * 8, 128)
    row1[...] = jnp.sum(jnp.where(diagonal(E * 8, 0), spread, 0.0), axis=0, keepdims=True)

    @pl.when(jnp.logical_not(is_owner))
    def _():
        pl.semaphore_wait(barrier, E)
        near = jnp.where(z < LINE // 4, half - 1 - z, 3 * half - 1 - z)
        pl.semaphore_signal(go_sem, inc=1, device_id=(s - z + near, x), device_id_type=MESH)

    @pl.when(is_owner)
    def _():
        pl.semaphore_wait(go_sem, 1)

    def to_owner(i):
        e = lax.rem(x + s + i, E)
        to = owner(e)

        @pl.when(to != s)
        def _():
            send(row1, rows1.at[pl.ds(s, 1)], 8, to, x)
            send(send1.at[e], recv1.at[s], 0, to, x)

        @pl.when(to == s)
        def _():
            keep(row1, rows1.at[pl.ds(s, 1)], 8)
            keep(send1.at[e], recv1.at[s], 0)

    each(E, to_owner)

    def sent_first():
        sent(send1.at[pl.ds(0, E - 1)], 0)
        each(E - 1, lambda i: sent(row1, 8))

        @pl.when(jnp.logical_not(is_owner))
        def _():
            sent(send1.at[0], 0)
            sent(row1, 8)

    pending.append(sent_first)

    @pl.when(is_owner)
    def _():
        wait_for(rows1, recv_sem.at[8])
        turned[...] = jnp.transpose(rows1[...])
        lses = turned[pl.ds(pl.multiple_of(mine * 8, 8), 8), :]
        top = jnp.max(lses, axis=1, keepdims=True)
        weights = jnp.exp(lses - top)
        total = jnp.sum(weights, axis=1, keepdims=True)
        weights = weights / total
        lse_keep[...] = jnp.broadcast_to(top + jnp.log(total), (8, 128))
        wait_for(recv1, recv_sem.at[0])
        slots = jnp.zeros((8, 128), f32)
        grads = jnp.zeros((8, 128), f32)
        for i in range(S):
            piece = recv1[i].astype(f32)
            slots = slots + weights[:, i : i + 1] * piece[0:8]
            grads = grads + piece[8:16]
        slot_keep[...] = slots
        send2[...] = jnp.concatenate([slots, grads], axis=0).astype(bf16)

        pl.semaphore_wait(barrier, S - both.astype(jnp.int32))
        each(S - 1, lambda i: send(send2, rows.at[x], 1, lax.rem(s + 1 + i, S), mine))

        @pl.when(jnp.logical_not(both))
        def _():
            send(send2, rows.at[x], 1, s, mine)

        @pl.when(both)
        def _():
            keep(send2, rows.at[x], 1)

    def sent_rows():
        @pl.when(is_owner)
        def _():
            each(S - 1, lambda i: sent(send2, 1))

            @pl.when(jnp.logical_not(both))
            def _():
                sent(send2, 1)

    pending.append(sent_rows)
    loads[3].wait()
    loads[4].wait()
    wait_for(rows, recv_sem.at[1])
    held = jnp.concatenate([rows[i] for i in range(E)], axis=1)
    pre_act = dot(held, win[...], 1, 0)
    act_grad = dot(held, wout[...], 1, 1)
    activated, derivative = gelu_parts(pre_act[0:8])
    pre_grad = act_grad[8:16] * derivative
    stacked = jnp.concatenate([activated, pre_grad], axis=0).astype(bf16)
    out_part = dot(stacked, wout[...], 1, 0)
    back_part = dot(stacked, win[...], 1, 1)
    for i in range(E):
        cut = slice(i * 128, i * 128 + 128)
        send3[i] = jnp.concatenate([out_part[0:8, cut], back_part[8:16, cut]], axis=0).astype(bf16)

    def to_home(i):
        to = lax.rem(x + s + i, E)
        own = jnp.logical_and(both, to == x)

        @pl.when(jnp.logical_not(own))
        def _():
            send(send3.at[to], recv3.at[s], 2, home, to)

        @pl.when(own)
        def _():
            keep(send3.at[to], recv3.at[s], 2)

    each(E, to_home)

    def sent_parts():
        sent(send3.at[pl.ds(0, E - 1)], 2)

        @pl.when(jnp.logical_not(both))
        def _():
            sent(send3.at[0], 2)

    pending.append(sent_parts)

    blank = jnp.zeros((8, 128), f32)
    gwout[...] = dot(jnp.concatenate([blank, activated], axis=0).astype(bf16), held, 0, 0).astype(bf16)
    gwin[...] = dot(held, jnp.concatenate([pre_grad, blank], axis=0).astype(bf16), 0, 0).astype(bf16)
    store_out = pltpu.make_async_copy(gwout, gwout_h, out_sem.at[0])
    store_in = pltpu.make_async_copy(gwin, gwin_h, out_sem.at[1])
    store_out.start()
    store_in.start()

    @pl.when(is_owner)
    def _():
        wait_for(recv3, recv_sem.at[2])
        total = lax.fori_loop(0, S, lambda i, t: t + recv3[i].astype(f32), jnp.zeros((16, 128), f32))
        send4[...] = total.astype(bf16)
        stat = jnp.sum(total[8:16].astype(bf16).astype(f32) * slot_keep[...], axis=1, keepdims=True)
        row4[...] = jnp.sum(
            jnp.where(diagonal(8, 0), lse_keep[...], jnp.where(diagonal(8, 8), stat, 0.0)), axis=0, keepdims=True
        )

        def to_line(i):
            to = lax.rem(s + 1 + i, S)
            send(row4, rows4.at[pl.ds(mine, 1)], 9, to, x)
            send(send4, recv4.at[mine], 3, to, x)

        each(S - 1, to_line)
        keep(row4, rows4.at[pl.ds(mine, 1)], 9)
        keep(send4, recv4.at[mine], 3)

    def sent_sums():
        @pl.when(is_owner)
        def _():
            each(S - 1, lambda i: sent(send4, 3))
            each(S - 1, lambda i: sent(row4, 9))

    pending.append(sent_sums)
    wait_for(recv4, recv_sem.at[3])
    wait_for(rows4, recv_sem.at[9])
    sums = recv4[...].astype(f32)
    outs = jnp.swapaxes(sums[:, 0:8, :], 0, 1).astype(bf16)
    backs = jnp.swapaxes(sums[:, 8:16, :], 0, 1).astype(bf16)
    scales = rows4[...]
    for c in range(C):
        comb_grad = dot(outs[c], grad[c], 1, 1)
        disp_grad = dot(backs[c], tokens[c], 1, 1)
        dispatch = jnp.exp(logits[c] - scales[:, c : c + 1])
        share = comb[c]
        disp[c] = dispatch
        part = share * (
            comb_grad - jnp.sum(share * comb_grad, axis=0, keepdims=True)
        ) + dispatch * (disp_grad - scales[:, C + c : C + c + 1])
        send5[c] = part.astype(bf16)

    def to_peer(i):
        to = lax.rem(q + 1 + i, Q)
        send(send5.at[pl.ds(to * per, per)], recv5.at[q], 4, s, side + to)

    each(Q - 1, to_peer)
    pending.append(lambda: sent(recv5.at[pl.ds(0, Q - 1)], 4))
    keep(send5.at[pl.ds(q * per, per)], recv5.at[q], 4)
    wait_for(recv5, recv_sem.at[4])
    part = recv5[0].astype(f32)
    for i in range(1, Q):
        part = part + recv5[i].astype(f32)
    send6[...] = part
    send(send6, recv6, 5, s, across)
    pending.append(lambda: sent(send6, 5))
    wait_for(recv6, recv_sem.at[5])
    recv7[q] = (send6[...] + recv6[...]).astype(bf16)
    each(Q - 1, lambda i: send(recv7.at[q], recv7.at[q], 6, s, side + lax.rem(q + 1 + i, Q)))
    pending.append(lambda: sent(recv7.at[pl.ds(0, Q - 1)], 6))
    loads[5].wait()
    wait_for(recv7.at[pl.ds(0, Q - 1)], recv_sem.at[6])

    term = jnp.zeros((E, 128), f32)
    for c in range(C):
        term = term + dot(recv7[c // per, c % per], tokens[c], 1, 0)
    recv8[s] = term.astype(bf16)
    each(S - 1, lambda i: send(recv8.at[s], recv8.at[s], 7, lax.rem(s + 1 + i, S), x))
    pending.append(lambda: sent(recv8.at[pl.ds(0, S - 1)], 7))

    for c in range(C):
        left = jnp.concatenate([disp[c].astype(bf16), recv7[c // per, c % per]], axis=0)
        right = jnp.concatenate([backs[c], params[...]], axis=0)
        gtok[c] = dot(left, right, 0, 0).astype(bf16)
    store_tok = pltpu.make_async_copy(gtok, gtok_h, out_sem.at[2])
    store_tok.start()

    wait_for(recv8.at[pl.ds(0, S - 1)], recv_sem.at[7])
    total = recv8[0].astype(f32)
    for i in range(1, S):
        total = total + recv8[i].astype(f32)
    gslot[...] = total
    store_slot = pltpu.make_async_copy(gslot, gslot_h, out_sem.at[3])
    store_slot.start()

    for wait in pending:
        wait()
    store_out.wait()
    store_in.wait()
    store_tok.wait()
    store_slot.wait()


def hand_over(*refs):
    sources, targets, held, sem = refs[0:4], refs[4:8], refs[8:12], refs[12]
    ins = [pltpu.make_async_copy(sources[i], held[i], sem.at[i]) for i in range(4)]
    outs = [pltpu.make_async_copy(held[i], targets[i], sem.at[4 + i]) for i in range(4)]
    for copy in ins:
        copy.start()
    for i in range(4):
        ins[i].wait()
        outs[i].start()
    for copy in outs:
        copy.wait()


def solution(mesh):
    S, E = mesh.shape["seq"], mesh.shape["exp"]

    def body(tokens, grad_out, logits, slot_params, weight_in, weight_out):
        C, M, D = tokens.shape
        _, wide, F = weight_in.shape
        args = (tokens, grad_out, logits, slot_params, weight_in[0], weight_out[0])
        outs = (
            jax.ShapeDtypeStruct((C, M, D), bf16),
            jax.ShapeDtypeStruct((E, D), f32),
            jax.ShapeDtypeStruct((wide, F), bf16),
            jax.ShapeDtypeStruct((F, wide), bf16),
        )
        Q = E // 2
        per = C // Q
        hold = lambda a: pltpu.VMEM(a.shape, a.dtype)
        scratch = (
            [hold(a) for a in args]
            + [hold(a) for a in outs]
            + [
                pltpu.VMEM((C, E, M), f32),
                pltpu.VMEM((C, E, M), f32),
                pltpu.VMEM((E, 16, D), bf16),
                pltpu.VMEM((S, 16, D), bf16),
                pltpu.VMEM((16, D), bf16),
                pltpu.VMEM((E, 16, D), bf16),
                pltpu.VMEM((E, 16, D), bf16),
                pltpu.VMEM((S, 16, D), bf16),
                pltpu.VMEM((16, D), bf16),
                pltpu.VMEM((E, 16, D), bf16),
                pltpu.VMEM((1, 128), f32),
                pltpu.VMEM((S, 128), f32),
                pltpu.VMEM((1, 128), f32),
                pltpu.VMEM((E, 128), f32),
                pltpu.VMEM((128, S), f32),
                pltpu.VMEM((C, E, M), bf16),
                pltpu.VMEM((Q, per, E, M), bf16),
                pltpu.VMEM((per, E, M), f32),
                pltpu.VMEM((per, E, M), f32),
                pltpu.VMEM((Q, per, E, M), bf16),
                pltpu.VMEM((S, E, D), bf16),
                pltpu.VMEM((8, D), f32),
                pltpu.VMEM((8, D), f32),
                pltpu.SemaphoreType.DMA((6,)),
                pltpu.SemaphoreType.DMA((4,)),
                pltpu.SemaphoreType.DMA((10,)),
                pltpu.SemaphoreType.DMA((10,)),
                pltpu.SemaphoreType.REGULAR,
            ]
        )
        gtok, gslot, gwin, gwout = pl.pallas_call(
            functools.partial(kernel, S, E, C),
            out_shape=outs,
            in_specs=[pl.BlockSpec(memory_space=pltpu.HBM)] * 6,
            out_specs=[pl.BlockSpec(memory_space=pl.ANY)] * 4,
            scratch_shapes=scratch,
            compiler_params=pltpu.CompilerParams(
                collective_id=0, has_side_effects=True, vmem_limit_bytes=60 << 20
            ),
            name="moe_backward",
        )(*args)
        gtok, gslot, gwin, gwout = pl.pallas_call(
            hand_over,
            out_shape=outs,
            in_specs=[pl.BlockSpec(memory_space=pl.ANY)] * 4,
            out_specs=[pl.BlockSpec(memory_space=pltpu.HBM)] * 4,
            scratch_shapes=[hold(a) for a in outs] + [pltpu.SemaphoreType.DMA((8,))],
            name="hand_over",
        )(gtok, gslot, gwin, gwout)
        return gtok, gslot, gwin[None], gwout[None]

    in_specs = (
        P(None, "seq", "exp"),
        P(None, "seq", "exp"),
        P(None, None, "seq"),
        P(None, "exp"),
        P("exp", None, "seq"),
        P("exp", "seq", None),
    )
    out_specs = (
        P(None, "seq", "exp"),
        P(None, "exp"),
        P("exp", None, "seq"),
        P("exp", "seq", None),
    )
    return jax.shard_map(body, mesh=mesh, in_specs=in_specs, out_specs=out_specs, check_vma=False)
```

```python
import functools

import jax
import jax.numpy as jnp
from jax import lax
from jax.experimental import pallas as pl
from jax.experimental.pallas import tpu as pltpu
from jax.sharding import PartitionSpec as P

root_coef = 0.7978845608028654
cubic_coef = 0.044715
MESH = pl.DeviceIdType.MESH
f32 = jnp.float32
bf16 = jnp.bfloat16
LINE = 8


def gelu_parts(pre_act):
    tanh_value = jnp.tanh(root_coef * (pre_act + cubic_coef * pre_act * pre_act * pre_act))
    activated = 0.5 * pre_act * (1.0 + tanh_value)
    derivative = 0.5 * (1.0 + tanh_value) + 0.5 * pre_act * (
        1.0 - tanh_value * tanh_value
    ) * root_coef * (1.0 + 3.0 * cubic_coef * pre_act * pre_act)
    return (activated, derivative)


def dot(a, b, ca, cb):
    return lax.dot_general(a, b, (((ca,), (cb,)), ((), ())), preferred_element_type=f32)


def wait_for(ref, sem):
    pltpu.make_async_copy(ref, ref, sem).wait()


def each(count, step):
    def run(i, carry):
        step(i)
        return carry

    lax.fori_loop(0, count, run, 0)


def kernel(
    S, E, C,
    tokens_h, grad_h, logits_h, params_h, win_h, wout_h,
    gtok_h, gslot_h, gwin_h, gwout_h,
    tokens, grad, logits, params, win, wout,
    gtok, gslot, gwin, gwout,
    comb, disp,
    send1, recv1, send2, rows, send3, recv3, send4, recv4,
    row1, rows1, row4, rows4, turned,
    send5, recv5, send6, recv6, recv7, recv8,
    slot_keep, lse_keep,
    in_sem, out_sem, send_sem, recv_sem, go_sem,
):
    s = lax.axis_index("seq")
    x = lax.axis_index("exp")
    half = LINE // 2
    Q = E // 2
    per = C // Q
    q = lax.rem(x, Q)
    side = x - q
    across = lax.rem(x + Q, E)

    def owner(e):
        return lax.div(e, half) * LINE + LINE // 4 + lax.rem(e, half)

    z = lax.rem(s, LINE)
    lines = S // LINE

    def swing(i):
        return jnp.where(lax.rem(i, 2) == 1, lax.div(i + 1, 2), -lax.div(i + 1, 2))

    def far_line(i):
        return lax.rem(lax.div(s, LINE) + lines // 2 + swing(lax.rem(i, lines)) + lines, lines)

    def far_ring(i, start):
        return far_line(i) * LINE + lax.rem(z + start + swing(lax.div(i, lines)) + LINE, LINE)

    def far_end(i):
        k = lax.div(i, lines)
        return far_line(i) * LINE + jnp.where(z < half, LINE - 1 - k, k)

    is_owner = jnp.logical_and(z >= LINE // 4, z < LINE // 4 + half)
    mine = lax.div(s, LINE) * half + jnp.clip(z - LINE // 4, 0, half - 1)
    both = jnp.logical_and(is_owner, mine == x)
    home = owner(x)

    loads = []
    for i, (a, b) in enumerate(
        ((logits_h, logits), (tokens_h, tokens), (grad_h, grad), (win_h, win), (wout_h, wout), (params_h, params))
    ):
        copy = pltpu.make_async_copy(a, b, in_sem.at[i])
        copy.start()
        loads.append(copy)

    barrier = pltpu.get_barrier_semaphore()

    def greet(ds, dx):
        pl.semaphore_signal(barrier, inc=1, device_id=(ds, dx), device_id_type=MESH)

    @pl.when(is_owner)
    def _():
        def to_rest(i):
            k = lax.rem(i + s, S - E)
            zz = lax.rem(k, half)
            greet(lax.div(k, half) * LINE + jnp.where(zz < LINE // 4, zz, zz + half), x)

        each(S - E, to_rest)

    def to_far(i):
        to = lax.rem(x + Q + i, E)

        @pl.when(jnp.logical_or(jnp.logical_not(both), to != x))
        def _():
            greet(home, to)

    each(E, to_far)

    def send(src, dst, k, ds, dx):
        pltpu.make_async_remote_copy(
            src_ref=src, dst_ref=dst, send_sem=send_sem.at[k], recv_sem=recv_sem.at[k],
            device_id=(ds, dx), device_id_type=MESH,
        ).start()

    def keep(src, dst, k):
        pltpu.make_async_copy(src, dst, recv_sem.at[k]).start()

    pending = []

    def sent(ref, k):
        wait_for(ref, send_sem.at[k])

    def diagonal(count, shift):
        down = lax.broadcasted_iota(jnp.int32, (count, 128), 0)
        along = lax.broadcasted_iota(jnp.int32, (count, 128), 1)
        return along == down + shift

    loads[0].wait()
    loads[1].wait()
    loads[2].wait()
    slot_parts, grad_parts, lse_parts = [], [], []
    for c in range(C):
        value = logits[c]
        top = jnp.max(value, axis=1, keepdims=True)
        weight = jnp.exp(value - top)
        mass = jnp.sum(weight, axis=1, keepdims=True)
        slot_parts.append(dot((weight / mass).astype(bf16), tokens[c], 1, 0))
        lse_parts.append(jnp.broadcast_to(top + jnp.log(mass), (E, 128)))
        crest = jnp.max(value, axis=0, keepdims=True)
        share = jnp.exp(value - crest)
        share = share / jnp.sum(share, axis=0, keepdims=True)
        comb[c] = share
        grad_parts.append(dot(share.astype(bf16), grad[c], 1, 0))
    send1[...] = jnp.concatenate(
        [jnp.swapaxes(jnp.stack(slot_parts), 0, 1), jnp.swapaxes(jnp.stack(grad_parts), 0, 1)], axis=1
    ).astype(bf16)
    spread = jnp.swapaxes(jnp.stack(lse_parts), 0, 1).reshape(E * 8, 128)
    row1[...] = jnp.sum(jnp.where(diagonal(E * 8, 0), spread, 0.0), axis=0, keepdims=True)

    @pl.when(jnp.logical_not(is_owner))
    def _():
        pl.semaphore_wait(barrier, E)

        def go(first):
            for i in range(half // 2):
                to = s - z + first + i
                pl.semaphore_signal(go_sem, inc=1, device_id=(to, x), device_id_type=MESH)

        @pl.when(z == LINE // 4 - 1)
        def _():
            go(LINE // 4)

        @pl.when(z == LINE // 4 + half)
        def _():
            go(LINE // 4 + half // 2)

    @pl.when(is_owner)
    def _():
        pl.semaphore_wait(go_sem, 1)

    def to_owner(i):
        k = lax.div(i, lines)
        e = far_line(i) * half + jnp.where(z < half, half - 1 - k, k)
        to = owner(e)

        @pl.when(to != s)
        def _():
            send(row1, rows1.at[pl.ds(s, 1)], 8, to, x)
            send(send1.at[e], recv1.at[s], 0, to, x)

        @pl.when(to == s)
        def _():
            keep(row1, rows1.at[pl.ds(s, 1)], 8)
            keep(send1.at[e], recv1.at[s], 0)

    each(E, to_owner)

    def sent_first():
        sent(send1.at[pl.ds(0, E - 1)], 0)
        each(E - 1, lambda i: sent(row1, 8))

        @pl.when(jnp.logical_not(is_owner))
        def _():
            sent(send1.at[0], 0)
            sent(row1, 8)

    pending.append(sent_first)

    @pl.when(is_owner)
    def _():
        wait_for(rows1, recv_sem.at[8])
        turned[...] = jnp.transpose(rows1[...])
        lses = turned[pl.ds(pl.multiple_of(mine * 8, 8), 8), :]
        top = jnp.max(lses, axis=1, keepdims=True)
        weights = jnp.exp(lses - top)
        total = jnp.sum(weights, axis=1, keepdims=True)
        weights = weights / total
        lse_keep[...] = jnp.broadcast_to(top + jnp.log(total), (8, 128))
        wait_for(recv1, recv_sem.at[0])
        slots = jnp.zeros((8, 128), f32)
        grads = jnp.zeros((8, 128), f32)
        for i in range(S):
            piece = recv1[i].astype(f32)
            slots = slots + weights[:, i : i + 1] * piece[0:8]
            grads = grads + piece[8:16]
        slot_keep[...] = slots
        send2[...] = jnp.concatenate([slots, grads], axis=0).astype(bf16)

        pl.semaphore_wait(barrier, S - both.astype(jnp.int32))
        start = jnp.where(lax.div(mine, Q) == lax.div(x, Q), half, 0)

        def to_expert(i):
            to = far_ring(i, start)
            own = jnp.logical_and(both, to == s)

            @pl.when(jnp.logical_not(own))
            def _():
                send(send2, rows.at[x], 1, to, mine)

            @pl.when(own)
            def _():
                keep(send2, rows.at[x], 1)

        each(S, to_expert)

    def sent_rows():
        @pl.when(is_owner)
        def _():
            each(S - 1, lambda i: sent(send2, 1))

            @pl.when(jnp.logical_not(both))
            def _():
                sent(send2, 1)

    pending.append(sent_rows)
    loads[3].wait()
    loads[4].wait()
    wait_for(rows, recv_sem.at[1])
    held = jnp.concatenate([rows[i] for i in range(E)], axis=1)
    pre_act = dot(held, win[...], 1, 0)
    act_grad = dot(held, wout[...], 1, 1)
    activated, derivative = gelu_parts(pre_act[0:8])
    pre_grad = act_grad[8:16] * derivative
    stacked = jnp.concatenate([activated, pre_grad], axis=0).astype(bf16)
    out_part = dot(stacked, wout[...], 1, 0)
    back_part = dot(stacked, win[...], 1, 1)
    for i in range(E):
        cut = slice(i * 128, i * 128 + 128)
        send3[i] = jnp.concatenate([out_part[0:8, cut], back_part[8:16, cut]], axis=0).astype(bf16)

    def to_home(i):
        to = jnp.where(i < Q, Q - side, side) + lax.rem(q + Q // 2 + swing(lax.rem(i, Q)) + Q, Q)
        own = jnp.logical_and(both, to == x)

        @pl.when(jnp.logical_not(own))
        def _():
            send(send3.at[to], recv3.at[s], 2, home, to)

        @pl.when(own)
        def _():
            keep(send3.at[to], recv3.at[s], 2)

    each(E, to_home)

    def sent_parts():
        sent(send3.at[pl.ds(0, E - 1)], 2)

        @pl.when(jnp.logical_not(both))
        def _():
            sent(send3.at[0], 2)

    pending.append(sent_parts)

    blank = jnp.zeros((8, 128), f32)
    gwout[...] = dot(jnp.concatenate([blank, activated], axis=0).astype(bf16), held, 0, 0).astype(bf16)
    gwin[...] = dot(held, jnp.concatenate([pre_grad, blank], axis=0).astype(bf16), 0, 0).astype(bf16)
    store_out = pltpu.make_async_copy(gwout, gwout_h, out_sem.at[0])
    store_in = pltpu.make_async_copy(gwin, gwin_h, out_sem.at[1])
    store_out.start()
    store_in.start()

    @pl.when(is_owner)
    def _():
        wait_for(recv3, recv_sem.at[2])
        total = lax.fori_loop(0, S, lambda i, t: t + recv3[i].astype(f32), jnp.zeros((16, 128), f32))
        send4[...] = total.astype(bf16)
        stat = jnp.sum(total[8:16].astype(bf16).astype(f32) * slot_keep[...], axis=1, keepdims=True)
        row4[...] = jnp.sum(
            jnp.where(diagonal(8, 0), lse_keep[...], jnp.where(diagonal(8, 8), stat, 0.0)), axis=0, keepdims=True
        )

        def to_line(i):
            to = far_ring(i, half)
            send(row4, rows4.at[pl.ds(mine, 1)], 9, to, x)
            send(send4, recv4.at[mine], 3, to, x)

        each(S - 1, to_line)
        keep(row4, rows4.at[pl.ds(mine, 1)], 9)
        keep(send4, recv4.at[mine], 3)

    def sent_sums():
        @pl.when(is_owner)
        def _():
            each(S - 1, lambda i: sent(send4, 3))
            each(S - 1, lambda i: sent(row4, 9))

    pending.append(sent_sums)
    wait_for(recv4, recv_sem.at[3])
    wait_for(rows4, recv_sem.at[9])
    sums = recv4[...].astype(f32)
    outs = jnp.swapaxes(sums[:, 0:8, :], 0, 1).astype(bf16)
    backs = jnp.swapaxes(sums[:, 8:16, :], 0, 1).astype(bf16)
    scales = rows4[...]
    for c in range(C):
        comb_grad = dot(outs[c], grad[c], 1, 1)
        disp_grad = dot(backs[c], tokens[c], 1, 1)
        dispatch = jnp.exp(logits[c] - scales[:, c : c + 1])
        share = comb[c]
        disp[c] = dispatch
        part = share * (
            comb_grad - jnp.sum(share * comb_grad, axis=0, keepdims=True)
        ) + dispatch * (disp_grad - scales[:, C + c : C + c + 1])
        send5[c] = part.astype(bf16)

    def to_peer(i):
        to = lax.rem(q + 1 + i, Q)
        send(send5.at[pl.ds(to * per, per)], recv5.at[q], 4, s, side + to)

    each(Q - 1, to_peer)
    pending.append(lambda: sent(recv5.at[pl.ds(0, Q - 1)], 4))
    keep(send5.at[pl.ds(q * per, per)], recv5.at[q], 4)
    wait_for(recv5, recv_sem.at[4])
    part = recv5[0].astype(f32)
    for i in range(1, Q):
        part = part + recv5[i].astype(f32)
    send6[...] = part
    send(send6, recv6, 5, s, across)
    pending.append(lambda: sent(send6, 5))
    wait_for(recv6, recv_sem.at[5])
    recv7[q] = (send6[...] + recv6[...]).astype(bf16)
    each(Q - 1, lambda i: send(recv7.at[q], recv7.at[q], 6, s, side + lax.rem(q + 1 + i, Q)))
    pending.append(lambda: sent(recv7.at[pl.ds(0, Q - 1)], 6))
    loads[5].wait()
    wait_for(recv7.at[pl.ds(0, Q - 1)], recv_sem.at[6])

    wide = jnp.concatenate([recv7[c // per, c % per] for c in range(C)], axis=1)
    term = dot(wide, tokens[...].reshape(wide.shape[1], 128), 1, 0)
    recv8[s] = term.astype(bf16)

    def to_plane(i):
        to = far_end(i)

        @pl.when(to != s)
        def _():
            send(recv8.at[s], recv8.at[s], 7, to, x)

    each(S, to_plane)
    pending.append(lambda: sent(recv8.at[pl.ds(0, S - 1)], 7))

    for c in range(C):
        left = jnp.concatenate([disp[c].astype(bf16), recv7[c // per, c % per]], axis=0)
        right = jnp.concatenate([backs[c], params[...]], axis=0)
        gtok[c] = dot(left, right, 0, 0).astype(bf16)
    store_tok = pltpu.make_async_copy(gtok, gtok_h, out_sem.at[2])
    store_tok.start()

    wait_for(recv8.at[pl.ds(0, S - 1)], recv_sem.at[7])
    total = recv8[0].astype(f32)
    for i in range(1, S):
        total = total + recv8[i].astype(f32)
    gslot[...] = total
    store_slot = pltpu.make_async_copy(gslot, gslot_h, out_sem.at[3])
    store_slot.start()

    for wait in pending:
        wait()
    store_out.wait()
    store_in.wait()
    store_tok.wait()
    store_slot.wait()


def hand_over(*refs):
    sources, targets, held, sem = refs[0:4], refs[4:8], refs[8:12], refs[12]
    ins = [pltpu.make_async_copy(sources[i], held[i], sem.at[i]) for i in range(4)]
    outs = [pltpu.make_async_copy(held[i], targets[i], sem.at[4 + i]) for i in range(4)]
    for copy in ins:
        copy.start()
    for i in range(4):
        ins[i].wait()
        outs[i].start()
    for copy in outs:
        copy.wait()


def solution(mesh):
    S, E = mesh.shape["seq"], mesh.shape["exp"]

    def body(tokens, grad_out, logits, slot_params, weight_in, weight_out):
        C, M, D = tokens.shape
        _, wide, F = weight_in.shape
        args = (tokens, grad_out, logits, slot_params, weight_in[0], weight_out[0])
        outs = (
            jax.ShapeDtypeStruct((C, M, D), bf16),
            jax.ShapeDtypeStruct((E, D), f32),
            jax.ShapeDtypeStruct((wide, F), bf16),
            jax.ShapeDtypeStruct((F, wide), bf16),
        )
        Q = E // 2
        per = C // Q
        hold = lambda a: pltpu.VMEM(a.shape, a.dtype)
        scratch = (
            [hold(a) for a in args]
            + [hold(a) for a in outs]
            + [
                pltpu.VMEM((C, E, M), f32),
                pltpu.VMEM((C, E, M), f32),
                pltpu.VMEM((E, 16, D), bf16),
                pltpu.VMEM((S, 16, D), bf16),
                pltpu.VMEM((16, D), bf16),
                pltpu.VMEM((E, 16, D), bf16),
                pltpu.VMEM((E, 16, D), bf16),
                pltpu.VMEM((S, 16, D), bf16),
                pltpu.VMEM((16, D), bf16),
                pltpu.VMEM((E, 16, D), bf16),
                pltpu.VMEM((1, 128), f32),
                pltpu.VMEM((S, 128), f32),
                pltpu.VMEM((1, 128), f32),
                pltpu.VMEM((E, 128), f32),
                pltpu.VMEM((128, S), f32),
                pltpu.VMEM((C, E, M), bf16),
                pltpu.VMEM((Q, per, E, M), bf16),
                pltpu.VMEM((per, E, M), f32),
                pltpu.VMEM((per, E, M), f32),
                pltpu.VMEM((Q, per, E, M), bf16),
                pltpu.VMEM((S, E, D), bf16),
                pltpu.VMEM((8, D), f32),
                pltpu.VMEM((8, D), f32),
                pltpu.SemaphoreType.DMA((6,)),
                pltpu.SemaphoreType.DMA((4,)),
                pltpu.SemaphoreType.DMA((10,)),
                pltpu.SemaphoreType.DMA((10,)),
                pltpu.SemaphoreType.REGULAR,
            ]
        )
        gtok, gslot, gwin, gwout = pl.pallas_call(
            functools.partial(kernel, S, E, C),
            out_shape=outs,
            in_specs=[pl.BlockSpec(memory_space=pltpu.HBM)] * 6,
            out_specs=[pl.BlockSpec(memory_space=pl.ANY)] * 4,
            scratch_shapes=scratch,
            compiler_params=pltpu.CompilerParams(
                collective_id=0, has_side_effects=True, vmem_limit_bytes=60 << 20
            ),
            name="moe_backward",
        )(*args)
        gtok, gslot, gwin, gwout = pl.pallas_call(
            hand_over,
            out_shape=outs,
            in_specs=[pl.BlockSpec(memory_space=pl.ANY)] * 4,
            out_specs=[pl.BlockSpec(memory_space=pltpu.HBM)] * 4,
            scratch_shapes=[hold(a) for a in outs] + [pltpu.SemaphoreType.DMA((8,))],
            name="hand_over",
        )(gtok, gslot, gwin, gwout)
        return gtok, gslot, gwin[None], gwout[None]

    in_specs = (
        P(None, "seq", "exp"),
        P(None, "seq", "exp"),
        P(None, None, "seq"),
        P(None, "exp"),
        P("exp", None, "seq"),
        P("exp", "seq", None),
    )
    out_specs = (
        P(None, "seq", "exp"),
        P(None, "exp"),
        P("exp", None, "seq"),
        P("exp", "seq", None),
    )
    return jax.shard_map(body, mesh=mesh, in_specs=in_specs, out_specs=out_specs, check_vma=False)
```

```python
import functools

import jax
import jax.numpy as jnp
from jax import lax
from jax.experimental import pallas as pl
from jax.experimental.pallas import tpu as pltpu
from jax.sharding import PartitionSpec as P

root_coef = 0.7978845608028654
cubic_coef = 0.044715
MESH = pl.DeviceIdType.MESH
f32 = jnp.float32
bf16 = jnp.bfloat16
LINE = 8


def gelu_parts(pre_act):
    tanh_value = jnp.tanh(root_coef * (pre_act + cubic_coef * pre_act * pre_act * pre_act))
    activated = 0.5 * pre_act * (1.0 + tanh_value)
    derivative = 0.5 * (1.0 + tanh_value) + 0.5 * pre_act * (
        1.0 - tanh_value * tanh_value
    ) * root_coef * (1.0 + 3.0 * cubic_coef * pre_act * pre_act)
    return (activated, derivative)


def dot(a, b, ca, cb):
    return lax.dot_general(a, b, (((ca,), (cb,)), ((), ())), preferred_element_type=f32)


def wait_for(ref, sem):
    pltpu.make_async_copy(ref, ref, sem).wait()


def each(count, step):
    def run(i, carry):
        step(i)
        return carry

    lax.fori_loop(0, count, run, 0)


def kernel(
    S, E, C,
    tokens_h, grad_h, logits_h, params_h, win_h, wout_h,
    gtok_h, gslot_h, gwin_h, gwout_h,
    tokens, grad, logits, params, win, wout,
    gtok, gslot, gwin, gwout,
    comb, disp,
    send1, recv1, send2, rows, send3, recv3, send4, recv4,
    row1, rows1, row4, rows4, turned,
    send5, pair, summed, recv5, recv7, recv8,
    slot_keep, lse_keep,
    in_sem, out_sem, send_sem, recv_sem, go_sem,
):
    s = lax.axis_index("seq")
    x = lax.axis_index("exp")
    half = LINE // 2
    Q = E // 2
    per = C // Q
    q = lax.rem(x, Q)
    side = x - q
    across = lax.rem(x + Q, E)

    def owner(e):
        return lax.div(e, half) * LINE + LINE // 4 + lax.rem(e, half)

    z = lax.rem(s, LINE)
    lines = S // LINE

    def swing(i):
        return jnp.where(lax.rem(i, 2) == 1, lax.div(i + 1, 2), -lax.div(i + 1, 2))

    def far_line(i):
        return lax.rem(lax.div(s, LINE) + lines // 2 + swing(lax.rem(i, lines)) + lines, lines)

    def far_ring(i, start):
        return far_line(i) * LINE + lax.rem(z + start + swing(lax.div(i, lines)) + LINE, LINE)

    def far_end(i):
        k = lax.div(i, lines)
        return far_line(i) * LINE + jnp.where(z < half, LINE - 1 - k, k)

    is_owner = jnp.logical_and(z >= LINE // 4, z < LINE // 4 + half)
    mine = lax.div(s, LINE) * half + jnp.clip(z - LINE // 4, 0, half - 1)
    both = jnp.logical_and(is_owner, mine == x)
    home = owner(x)

    barrier = pltpu.get_barrier_semaphore()

    def greet(ds, dx):
        pl.semaphore_signal(barrier, inc=1, device_id=(ds, dx), device_id_type=MESH)

    @pl.when(is_owner)
    def _():
        def to_rest(i):
            k = lax.rem(i + s, S - E)
            zz = lax.rem(k, half)
            greet(lax.div(k, half) * LINE + jnp.where(zz < LINE // 4, zz, zz + half), x)

        each(S - E, to_rest)

    def to_far(i):
        to = lax.rem(x + Q + i, E)

        @pl.when(jnp.logical_or(jnp.logical_not(both), to != x))
        def _():
            greet(home, to)

    each(E, to_far)

    loads = []
    for i, (a, b) in enumerate(
        ((logits_h, logits), (tokens_h, tokens), (grad_h, grad), (win_h, win), (wout_h, wout), (params_h, params))
    ):
        copy = pltpu.make_async_copy(a, b, in_sem.at[i])
        copy.start()
        loads.append(copy)

    def send(src, dst, k, ds, dx):
        pltpu.make_async_remote_copy(
            src_ref=src, dst_ref=dst, send_sem=send_sem.at[k], recv_sem=recv_sem.at[k],
            device_id=(ds, dx), device_id_type=MESH,
        ).start()

    def keep(src, dst, k):
        pltpu.make_async_copy(src, dst, recv_sem.at[k]).start()

    pending = []

    def sent(ref, k):
        wait_for(ref, send_sem.at[k])

    def diagonal(count, shift):
        down = lax.broadcasted_iota(jnp.int32, (count, 128), 0)
        along = lax.broadcasted_iota(jnp.int32, (count, 128), 1)
        return along == down + shift

    loads[0].wait()
    loads[1].wait()
    loads[2].wait()
    slot_parts, grad_parts, lse_parts = [], [], []
    for c in range(C):
        value = logits[c]
        top = jnp.max(value, axis=1, keepdims=True)
        weight = jnp.exp(value - top)
        mass = jnp.sum(weight, axis=1, keepdims=True)
        slot_parts.append(dot((weight / mass).astype(bf16), tokens[c], 1, 0))
        lse_parts.append(jnp.broadcast_to(top + jnp.log(mass), (E, 128)))
        crest = jnp.max(value, axis=0, keepdims=True)
        share = jnp.exp(value - crest)
        share = share / jnp.sum(share, axis=0, keepdims=True)
        comb[c] = share
        grad_parts.append(dot(share.astype(bf16), grad[c], 1, 0))
    send1[...] = jnp.concatenate(
        [jnp.swapaxes(jnp.stack(slot_parts), 0, 1), jnp.swapaxes(jnp.stack(grad_parts), 0, 1)], axis=1
    ).astype(bf16)
    spread = jnp.swapaxes(jnp.stack(lse_parts), 0, 1).reshape(E * 8, 128)
    row1[...] = jnp.sum(jnp.where(diagonal(E * 8, 0), spread, 0.0), axis=0, keepdims=True)

    @pl.when(jnp.logical_not(is_owner))
    def _():
        pl.semaphore_wait(barrier, E)

        def go(first):
            for i in range(half // 2):
                to = s - z + first + i
                pl.semaphore_signal(go_sem, inc=1, device_id=(to, x), device_id_type=MESH)

        @pl.when(z == LINE // 4 - 1)
        def _():
            go(LINE // 4)

        @pl.when(z == LINE // 4 + half)
        def _():
            go(LINE // 4 + half // 2)

    @pl.when(is_owner)
    def _():
        pl.semaphore_wait(go_sem, 1)

    def to_owner(i):
        k = lax.div(i, lines)
        e = far_line(i) * half + jnp.where(z < half, half - 1 - k, k)
        to = owner(e)

        @pl.when(to != s)
        def _():
            send(row1, rows1.at[pl.ds(s, 1)], 8, to, x)
            send(send1.at[e], recv1.at[s], 0, to, x)

        @pl.when(to == s)
        def _():
            keep(row1, rows1.at[pl.ds(s, 1)], 8)
            keep(send1.at[e], recv1.at[s], 0)

    each(E, to_owner)

    def sent_first():
        sent(send1.at[pl.ds(0, E - 1)], 0)
        each(E - 1, lambda i: sent(row1, 8))

        @pl.when(jnp.logical_not(is_owner))
        def _():
            sent(send1.at[0], 0)
            sent(row1, 8)

    pending.append(sent_first)

    @pl.when(is_owner)
    def _():
        wait_for(rows1, recv_sem.at[8])
        turned[...] = jnp.transpose(rows1[...])
        lses = turned[pl.ds(pl.multiple_of(mine * 8, 8), 8), :]
        top = jnp.max(lses, axis=1, keepdims=True)
        weights = jnp.exp(lses - top)
        total = jnp.sum(weights, axis=1, keepdims=True)
        weights = weights / total
        lse_keep[...] = jnp.broadcast_to(top + jnp.log(total), (8, 128))
        wait_for(recv1, recv_sem.at[0])
        slots = jnp.zeros((8, 128), f32)
        grads = jnp.zeros((8, 128), f32)
        for i in range(S):
            piece = recv1[i].astype(f32)
            slots = slots + weights[:, i : i + 1] * piece[0:8]
            grads = grads + piece[8:16]
        slot_keep[...] = slots
        send2[...] = jnp.concatenate([slots, grads], axis=0).astype(bf16)

        pl.semaphore_wait(barrier, S - both.astype(jnp.int32))
        start = jnp.where(lax.div(mine, Q) == lax.div(x, Q), half, 0)

        def to_expert(i):
            to = far_ring(i, start)
            own = jnp.logical_and(both, to == s)

            @pl.when(jnp.logical_not(own))
            def _():
                send(send2, rows.at[x], 1, to, mine)

            @pl.when(own)
            def _():
                keep(send2, rows.at[x], 1)

        each(S, to_expert)

    def sent_rows():
        @pl.when(is_owner)
        def _():
            each(S - 1, lambda i: sent(send2, 1))

            @pl.when(jnp.logical_not(both))
            def _():
                sent(send2, 1)

    pending.append(sent_rows)
    loads[3].wait()
    loads[4].wait()
    wait_for(rows, recv_sem.at[1])
    held = jnp.concatenate([rows[i] for i in range(E)], axis=1)
    pre_act = dot(held, win[...], 1, 0)
    act_grad = dot(held, wout[...], 1, 1)
    activated, derivative = gelu_parts(pre_act[0:8])
    pre_grad = act_grad[8:16] * derivative
    stacked = jnp.concatenate([activated, pre_grad], axis=0).astype(bf16)
    out_part = dot(stacked, wout[...], 1, 0)
    back_part = dot(stacked, win[...], 1, 1)
    for i in range(E):
        cut = slice(i * 128, i * 128 + 128)
        send3[i] = jnp.concatenate([out_part[0:8, cut], back_part[8:16, cut]], axis=0).astype(bf16)

    def to_home(i):
        to = jnp.where(i < Q, Q - side, side) + lax.rem(q + Q // 2 + swing(lax.rem(i, Q)) + Q, Q)
        own = jnp.logical_and(both, to == x)

        @pl.when(jnp.logical_not(own))
        def _():
            send(send3.at[to], recv3.at[s], 2, home, to)

        @pl.when(own)
        def _():
            keep(send3.at[to], recv3.at[s], 2)

    each(E, to_home)

    def sent_parts():
        sent(send3.at[pl.ds(0, E - 1)], 2)

        @pl.when(jnp.logical_not(both))
        def _():
            sent(send3.at[0], 2)

    pending.append(sent_parts)

    blank = jnp.zeros((8, 128), f32)
    gwout[...] = dot(jnp.concatenate([blank, activated], axis=0).astype(bf16), held, 0, 0).astype(bf16)
    gwin[...] = dot(held, jnp.concatenate([pre_grad, blank], axis=0).astype(bf16), 0, 0).astype(bf16)
    store_out = pltpu.make_async_copy(gwout, gwout_h, out_sem.at[0])
    store_in = pltpu.make_async_copy(gwin, gwin_h, out_sem.at[1])
    store_out.start()
    store_in.start()

    @pl.when(is_owner)
    def _():
        wait_for(recv3, recv_sem.at[2])
        sums = [recv3[i].astype(f32) for i in range(4)]
        for i in range(4, S):
            sums[i % 4] = sums[i % 4] + recv3[i].astype(f32)
        total = (sums[0] + sums[1]) + (sums[2] + sums[3])
        send4[...] = total.astype(bf16)
        stat = jnp.sum(total[8:16].astype(bf16).astype(f32) * slot_keep[...], axis=1, keepdims=True)
        row4[...] = jnp.sum(
            jnp.where(diagonal(8, 0), lse_keep[...], jnp.where(diagonal(8, 8), stat, 0.0)), axis=0, keepdims=True
        )

        def to_line(i):
            to = far_ring(i, half)
            send(row4, rows4.at[pl.ds(mine, 1)], 9, to, x)
            send(send4, recv4.at[mine], 3, to, x)

        each(S - 1, to_line)
        keep(row4, rows4.at[pl.ds(mine, 1)], 9)
        keep(send4, recv4.at[mine], 3)

    def sent_sums():
        @pl.when(is_owner)
        def _():
            each(S - 1, lambda i: sent(send4, 3))
            each(S - 1, lambda i: sent(row4, 9))

    pending.append(sent_sums)
    wait_for(recv4, recv_sem.at[3])
    wait_for(rows4, recv_sem.at[9])
    sums = recv4[...].astype(f32)
    outs = jnp.swapaxes(sums[:, 0:8, :], 0, 1).astype(bf16)
    backs = jnp.swapaxes(sums[:, 8:16, :], 0, 1).astype(bf16)
    scales = rows4[...]
    for c in range(C):
        comb_grad = dot(outs[c], grad[c], 1, 1)
        disp_grad = dot(backs[c], tokens[c], 1, 1)
        dispatch = jnp.exp(logits[c] - scales[:, c : c + 1])
        share = comb[c]
        disp[c] = dispatch
        part = share * (
            comb_grad - jnp.sum(share * comb_grad, axis=0, keepdims=True)
        ) + dispatch * (disp_grad - scales[:, C + c : C + c + 1])
        chunk = c // per
        send5[(chunk % 2 * (Q // 2) + chunk // 2) * per + c % per] = part.astype(bf16)

    core = lax.rem(x, 2)
    deep = C // 2
    pieces = Q // 2
    send(send5.at[pl.ds((1 - core) * deep, deep)], pair, 5, s, x + 1 - 2 * core)
    pending.append(lambda: sent(pair, 5))
    wait_for(pair, recv_sem.at[5])
    for i in range(pieces):
        own = send5[pl.ds(core * deep + i * per, per)].astype(f32)
        summed[i] = (own + pair[i * per : i * per + per].astype(f32)).astype(bf16)
    slot = lax.div(x, 2)

    def to_peer(i):
        to = lax.rem(lax.div(q, 2) + pieces // 2 + swing(lax.rem(i, pieces)) + pieces, pieces)
        send(summed.at[to], recv5.at[slot], 4, s, jnp.where(i < pieces, Q - side, side) + 2 * to + core)

    each(Q - 1, to_peer)
    pending.append(lambda: sent(recv5.at[pl.ds(0, Q - 1)], 4))
    keep(summed.at[lax.div(q, 2)], recv5.at[slot], 4)
    wait_for(recv5, recv_sem.at[4])
    part = recv5[0].astype(f32)
    for i in range(1, Q):
        part = part + recv5[i].astype(f32)
    recv7[q] = part.astype(bf16)
    each(Q - 1, lambda i: send(recv7.at[q], recv7.at[q], 6, s, side + lax.rem(q + 1 + i, Q)))
    pending.append(lambda: sent(recv7.at[pl.ds(0, Q - 1)], 6))
    loads[5].wait()
    wait_for(recv7.at[pl.ds(0, Q - 1)], recv_sem.at[6])

    wide = jnp.concatenate([recv7[c // per, c % per] for c in range(C)], axis=1)
    term = dot(wide, tokens[...].reshape(wide.shape[1], 128), 1, 0)
    recv8[s] = term.astype(bf16)

    def to_plane(i):
        to = far_end(i)

        @pl.when(to != s)
        def _():
            send(recv8.at[s], recv8.at[s], 7, to, x)

    each(S, to_plane)

    for c in range(C):
        left = jnp.concatenate([disp[c].astype(bf16), recv7[c // per, c % per]], axis=0)
        right = jnp.concatenate([backs[c], params[...]], axis=0)
        gtok[c] = dot(left, right, 0, 0).astype(bf16)
    store_tok = pltpu.make_async_copy(gtok, gtok_h, out_sem.at[2])
    store_tok.start()

    for wait in pending:
        wait()
    store_out.wait()
    store_in.wait()
    store_tok.wait()
    wait_for(recv8.at[pl.ds(0, S - 1)], recv_sem.at[7])
    total = recv8[0].astype(f32)
    for i in range(1, S):
        total = total + recv8[i].astype(f32)
    gslot[...] = total
    store_slot = pltpu.make_async_copy(gslot, gslot_h, out_sem.at[3])
    store_slot.start()

    sent(recv8.at[pl.ds(0, S - 1)], 7)
    store_slot.wait()


def hand_over(*refs):
    sources, targets, held, sem = refs[0:4], refs[4:8], refs[8:12], refs[12]
    ins = [pltpu.make_async_copy(sources[i], held[i], sem.at[i]) for i in range(4)]
    outs = [pltpu.make_async_copy(held[i], targets[i], sem.at[4 + i]) for i in range(4)]
    for copy in ins:
        copy.start()
    for i in range(4):
        ins[i].wait()
        outs[i].start()
    for copy in outs:
        copy.wait()


def solution(mesh):
    S, E = mesh.shape["seq"], mesh.shape["exp"]

    def body(tokens, grad_out, logits, slot_params, weight_in, weight_out):
        C, M, D = tokens.shape
        _, wide, F = weight_in.shape
        args = (tokens, grad_out, logits, slot_params, weight_in[0], weight_out[0])
        outs = (
            jax.ShapeDtypeStruct((C, M, D), bf16),
            jax.ShapeDtypeStruct((E, D), f32),
            jax.ShapeDtypeStruct((wide, F), bf16),
            jax.ShapeDtypeStruct((F, wide), bf16),
        )
        Q = E // 2
        per = C // Q
        hold = lambda a: pltpu.VMEM(a.shape, a.dtype)
        scratch = (
            [hold(a) for a in args]
            + [hold(a) for a in outs]
            + [
                pltpu.VMEM((C, E, M), f32),
                pltpu.VMEM((C, E, M), f32),
                pltpu.VMEM((E, 16, D), bf16),
                pltpu.VMEM((S, 16, D), bf16),
                pltpu.VMEM((16, D), bf16),
                pltpu.VMEM((E, 16, D), bf16),
                pltpu.VMEM((E, 16, D), bf16),
                pltpu.VMEM((S, 16, D), bf16),
                pltpu.VMEM((16, D), bf16),
                pltpu.VMEM((E, 16, D), bf16),
                pltpu.VMEM((1, 128), f32),
                pltpu.VMEM((S, 128), f32),
                pltpu.VMEM((1, 128), f32),
                pltpu.VMEM((E, 128), f32),
                pltpu.VMEM((128, S), f32),
                pltpu.VMEM((C, E, M), bf16),
                pltpu.VMEM((C // 2, E, M), bf16),
                pltpu.VMEM((Q // 2, per, E, M), bf16),
                pltpu.VMEM((Q, per, E, M), bf16),
                pltpu.VMEM((Q, per, E, M), bf16),
                pltpu.VMEM((S, E, D), bf16),
                pltpu.VMEM((8, D), f32),
                pltpu.VMEM((8, D), f32),
                pltpu.SemaphoreType.DMA((6,)),
                pltpu.SemaphoreType.DMA((4,)),
                pltpu.SemaphoreType.DMA((10,)),
                pltpu.SemaphoreType.DMA((10,)),
                pltpu.SemaphoreType.REGULAR,
            ]
        )
        gtok, gslot, gwin, gwout = pl.pallas_call(
            functools.partial(kernel, S, E, C),
            out_shape=outs,
            in_specs=[pl.BlockSpec(memory_space=pltpu.HBM)] * 6,
            out_specs=[pl.BlockSpec(memory_space=pl.ANY)] * 4,
            scratch_shapes=scratch,
            compiler_params=pltpu.CompilerParams(
                collective_id=0, has_side_effects=True, vmem_limit_bytes=60 << 20
            ),
            name="moe_backward",
        )(*args)
        gtok, gslot, gwin, gwout = pl.pallas_call(
            hand_over,
            out_shape=outs,
            in_specs=[pl.BlockSpec(memory_space=pl.ANY)] * 4,
            out_specs=[pl.BlockSpec(memory_space=pltpu.HBM)] * 4,
            scratch_shapes=[hold(a) for a in outs] + [pltpu.SemaphoreType.DMA((8,))],
            name="hand_over",
        )(gtok, gslot, gwin, gwout)
        return gtok, gslot, gwin[None], gwout[None]

    in_specs = (
        P(None, "seq", "exp"),
        P(None, "seq", "exp"),
        P(None, None, "seq"),
        P(None, "exp"),
        P("exp", None, "seq"),
        P("exp", "seq", None),
    )
    out_specs = (
        P(None, "seq", "exp"),
        P(None, "exp"),
        P("exp", None, "seq"),
        P("exp", "seq", None),
    )
    return jax.shard_map(body, mesh=mesh, in_specs=in_specs, out_specs=out_specs, check_vma=False)
```

```python
import functools

import jax
import jax.numpy as jnp
from jax import lax
from jax.experimental import pallas as pl
from jax.experimental.pallas import tpu as pltpu
from jax.sharding import PartitionSpec as P

root_coef = 0.7978845608028654
cubic_coef = 0.044715
MESH = pl.DeviceIdType.MESH
f32 = jnp.float32
bf16 = jnp.bfloat16
LINE = 8


def gelu_parts(pre_act):
    tanh_value = jnp.tanh(root_coef * (pre_act + cubic_coef * pre_act * pre_act * pre_act))
    activated = 0.5 * pre_act * (1.0 + tanh_value)
    derivative = 0.5 * (1.0 + tanh_value) + 0.5 * pre_act * (
        1.0 - tanh_value * tanh_value
    ) * root_coef * (1.0 + 3.0 * cubic_coef * pre_act * pre_act)
    return (activated, derivative)


def dot(a, b, ca, cb):
    return lax.dot_general(a, b, (((ca,), (cb,)), ((), ())), preferred_element_type=f32)


def wait_for(ref, sem):
    pltpu.make_async_copy(ref, ref, sem).wait()


def each(count, step):
    def run(i, carry):
        step(i)
        return carry

    lax.fori_loop(0, count, run, 0)


def kernel(
    S, E, C,
    tokens_h, grad_h, logits_h, params_h, win_h, wout_h,
    gtok_h, recv8, gwin_h, gwout_h,
    tokens, grad, logits, params, win, wout,
    gtok, term8, gwin, gwout,
    comb, disp,
    send1, recv1, send2, rows, send3, recv3, send4, recv4,
    row1, rows1, row4, rows4, turned,
    send5, pair, summed, recv5, recv7,
    slot_keep, lse_keep,
    in_sem, out_sem, send_sem, recv_sem, go_sem,
):
    s = lax.axis_index("seq")
    x = lax.axis_index("exp")
    half = LINE // 2
    Q = E // 2
    per = C // Q
    q = lax.rem(x, Q)
    side = x - q
    across = lax.rem(x + Q, E)

    def owner(e):
        return lax.div(e, half) * LINE + LINE // 4 + lax.rem(e, half)

    z = lax.rem(s, LINE)
    lines = S // LINE

    def swing(i):
        return jnp.where(lax.rem(i, 2) == 1, lax.div(i + 1, 2), -lax.div(i + 1, 2))

    def far_line(i):
        return lax.rem(lax.div(s, LINE) + lines // 2 + swing(lax.rem(i, lines)) + lines, lines)

    def far_ring(i, start):
        return far_line(i) * LINE + lax.rem(z + start + swing(lax.div(i, lines)) + LINE, LINE)

    def far_end(i):
        k = lax.div(i, lines)
        return far_line(i) * LINE + jnp.where(z < half, LINE - 1 - k, k)

    is_owner = jnp.logical_and(z >= LINE // 4, z < LINE // 4 + half)
    mine = lax.div(s, LINE) * half + jnp.clip(z - LINE // 4, 0, half - 1)
    both = jnp.logical_and(is_owner, mine == x)
    home = owner(x)

    barrier = pltpu.get_barrier_semaphore()

    def greet(ds, dx):
        pl.semaphore_signal(barrier, inc=1, device_id=(ds, dx), device_id_type=MESH)

    @pl.when(is_owner)
    def _():
        def to_rest(i):
            k = lax.rem(i + s, S - E)
            zz = lax.rem(k, half)
            greet(lax.div(k, half) * LINE + jnp.where(zz < LINE // 4, zz, zz + half), x)

        each(S - E, to_rest)

    def to_far(i):
        to = lax.rem(x + Q + i, E)

        @pl.when(jnp.logical_or(jnp.logical_not(both), to != x))
        def _():
            greet(home, to)

    each(E, to_far)

    loads = []
    for i, (a, b) in enumerate(
        ((logits_h, logits), (tokens_h, tokens), (grad_h, grad), (win_h, win), (wout_h, wout), (params_h, params))
    ):
        copy = pltpu.make_async_copy(a, b, in_sem.at[i])
        copy.start()
        loads.append(copy)

    def send(src, dst, k, ds, dx):
        pltpu.make_async_remote_copy(
            src_ref=src, dst_ref=dst, send_sem=send_sem.at[k], recv_sem=recv_sem.at[k],
            device_id=(ds, dx), device_id_type=MESH,
        ).start()

    def keep(src, dst, k):
        pltpu.make_async_copy(src, dst, recv_sem.at[k]).start()

    pending = []

    def sent(ref, k):
        wait_for(ref, send_sem.at[k])

    def diagonal(count, shift):
        down = lax.broadcasted_iota(jnp.int32, (count, 128), 0)
        along = lax.broadcasted_iota(jnp.int32, (count, 128), 1)
        return along == down + shift

    loads[0].wait()
    loads[1].wait()
    loads[2].wait()
    slot_parts, grad_parts, lse_parts = [], [], []
    for c in range(C):
        value = logits[c]
        top = jnp.max(value, axis=1, keepdims=True)
        weight = jnp.exp(value - top)
        mass = jnp.sum(weight, axis=1, keepdims=True)
        slot_parts.append(dot((weight / mass).astype(bf16), tokens[c], 1, 0))
        lse_parts.append(jnp.broadcast_to(top + jnp.log(mass), (E, 128)))
        crest = jnp.max(value, axis=0, keepdims=True)
        share = jnp.exp(value - crest)
        share = share / jnp.sum(share, axis=0, keepdims=True)
        comb[c] = share
        grad_parts.append(dot(share.astype(bf16), grad[c], 1, 0))
    send1[...] = jnp.concatenate(
        [jnp.swapaxes(jnp.stack(slot_parts), 0, 1), jnp.swapaxes(jnp.stack(grad_parts), 0, 1)], axis=1
    ).astype(bf16)
    spread = jnp.swapaxes(jnp.stack(lse_parts), 0, 1).reshape(E * 8, 128)
    row1[...] = jnp.sum(jnp.where(diagonal(E * 8, 0), spread, 0.0), axis=0, keepdims=True)

    @pl.when(jnp.logical_not(is_owner))
    def _():
        pl.semaphore_wait(barrier, E)

        def go(first):
            for i in range(half // 2):
                to = s - z + first + i
                pl.semaphore_signal(go_sem, inc=1, device_id=(to, x), device_id_type=MESH)

        @pl.when(z == LINE // 4 - 1)
        def _():
            go(LINE // 4)

        @pl.when(z == LINE // 4 + half)
        def _():
            go(LINE // 4 + half // 2)

    @pl.when(is_owner)
    def _():
        pl.semaphore_wait(go_sem, 1)

    def to_owner(i):
        k = lax.div(i, lines)
        e = far_line(i) * half + jnp.where(z < half, half - 1 - k, k)
        to = owner(e)

        @pl.when(to != s)
        def _():
            send(row1, rows1.at[pl.ds(s, 1)], 8, to, x)
            send(send1.at[e], recv1.at[s], 0, to, x)

        @pl.when(to == s)
        def _():
            keep(row1, rows1.at[pl.ds(s, 1)], 8)
            keep(send1.at[e], recv1.at[s], 0)

    each(E, to_owner)

    def sent_first():
        sent(send1.at[pl.ds(0, E - 1)], 0)
        each(E - 1, lambda i: sent(row1, 8))

        @pl.when(jnp.logical_not(is_owner))
        def _():
            sent(send1.at[0], 0)
            sent(row1, 8)

    pending.append(sent_first)

    @pl.when(is_owner)
    def _():
        wait_for(rows1, recv_sem.at[8])
        turned[...] = jnp.transpose(rows1[...])
        lses = turned[pl.ds(pl.multiple_of(mine * 8, 8), 8), :]
        top = jnp.max(lses, axis=1, keepdims=True)
        weights = jnp.exp(lses - top)
        total = jnp.sum(weights, axis=1, keepdims=True)
        weights = weights / total
        lse_keep[...] = jnp.broadcast_to(top + jnp.log(total), (8, 128))
        wait_for(recv1, recv_sem.at[0])
        slots = jnp.zeros((8, 128), f32)
        grads = jnp.zeros((8, 128), f32)
        for i in range(S):
            piece = recv1[i].astype(f32)
            slots = slots + weights[:, i : i + 1] * piece[0:8]
            grads = grads + piece[8:16]
        slot_keep[...] = slots
        send2[...] = jnp.concatenate([slots, grads], axis=0).astype(bf16)

        pl.semaphore_wait(barrier, S - both.astype(jnp.int32))
        start = jnp.where(lax.div(mine, Q) == lax.div(x, Q), half, 0)

        def to_expert(i):
            to = far_ring(i, start)
            own = jnp.logical_and(both, to == s)

            @pl.when(jnp.logical_not(own))
            def _():
                send(send2, rows.at[x], 1, to, mine)

            @pl.when(own)
            def _():
                keep(send2, rows.at[x], 1)

        each(S, to_expert)

    def sent_rows():
        @pl.when(is_owner)
        def _():
            each(S - 1, lambda i: sent(send2, 1))

            @pl.when(jnp.logical_not(both))
            def _():
                sent(send2, 1)

    pending.append(sent_rows)
    loads[3].wait()
    loads[4].wait()
    wait_for(rows, recv_sem.at[1])
    held = jnp.concatenate([rows[i] for i in range(E)], axis=1)
    pre_act = dot(held, win[...], 1, 0)
    act_grad = dot(held, wout[...], 1, 1)
    activated, derivative = gelu_parts(pre_act[0:8])
    pre_grad = act_grad[8:16] * derivative
    stacked = jnp.concatenate([activated, pre_grad], axis=0).astype(bf16)
    out_part = dot(stacked, wout[...], 1, 0)
    back_part = dot(stacked, win[...], 1, 1)
    for i in range(E):
        cut = slice(i * 128, i * 128 + 128)
        send3[i] = jnp.concatenate([out_part[0:8, cut], back_part[8:16, cut]], axis=0).astype(bf16)

    def to_home(i):
        to = jnp.where(i < Q, Q - side, side) + lax.rem(q + Q // 2 + swing(lax.rem(i, Q)) + Q, Q)
        own = jnp.logical_and(both, to == x)

        @pl.when(jnp.logical_not(own))
        def _():
            send(send3.at[to], recv3.at[s], 2, home, to)

        @pl.when(own)
        def _():
            keep(send3.at[to], recv3.at[s], 2)

    each(E, to_home)

    def sent_parts():
        sent(send3.at[pl.ds(0, E - 1)], 2)

        @pl.when(jnp.logical_not(both))
        def _():
            sent(send3.at[0], 2)

    pending.append(sent_parts)

    blank = jnp.zeros((8, 128), f32)
    gwout[...] = dot(jnp.concatenate([blank, activated], axis=0).astype(bf16), held, 0, 0).astype(bf16)
    gwin[...] = dot(held, jnp.concatenate([pre_grad, blank], axis=0).astype(bf16), 0, 0).astype(bf16)
    store_out = pltpu.make_async_copy(gwout, gwout_h, out_sem.at[0])
    store_in = pltpu.make_async_copy(gwin, gwin_h, out_sem.at[1])
    store_out.start()
    store_in.start()

    @pl.when(is_owner)
    def _():
        wait_for(recv3, recv_sem.at[2])
        sums = [recv3[i].astype(f32) for i in range(4)]
        for i in range(4, S):
            sums[i % 4] = sums[i % 4] + recv3[i].astype(f32)
        total = (sums[0] + sums[1]) + (sums[2] + sums[3])
        send4[...] = total.astype(bf16)
        stat = jnp.sum(total[8:16].astype(bf16).astype(f32) * slot_keep[...], axis=1, keepdims=True)
        row4[...] = jnp.sum(
            jnp.where(diagonal(8, 0), lse_keep[...], jnp.where(diagonal(8, 8), stat, 0.0)), axis=0, keepdims=True
        )

        def to_line(i):
            to = far_ring(i, half)
            send(row4, rows4.at[pl.ds(mine, 1)], 9, to, x)
            send(send4, recv4.at[mine], 3, to, x)

        each(S - 1, to_line)
        keep(row4, rows4.at[pl.ds(mine, 1)], 9)
        keep(send4, recv4.at[mine], 3)

    def sent_sums():
        @pl.when(is_owner)
        def _():
            each(S - 1, lambda i: sent(send4, 3))
            each(S - 1, lambda i: sent(row4, 9))

    pending.append(sent_sums)
    wait_for(recv4, recv_sem.at[3])
    wait_for(rows4, recv_sem.at[9])
    sums = recv4[...].astype(f32)
    outs = jnp.swapaxes(sums[:, 0:8, :], 0, 1).astype(bf16)
    backs = jnp.swapaxes(sums[:, 8:16, :], 0, 1).astype(bf16)
    scales = rows4[...]
    for c in range(C):
        comb_grad = dot(outs[c], grad[c], 1, 1)
        disp_grad = dot(backs[c], tokens[c], 1, 1)
        dispatch = jnp.exp(logits[c] - scales[:, c : c + 1])
        share = comb[c]
        disp[c] = dispatch
        part = share * (
            comb_grad - jnp.sum(share * comb_grad, axis=0, keepdims=True)
        ) + dispatch * (disp_grad - scales[:, C + c : C + c + 1])
        chunk = c // per
        send5[(chunk % 2 * (Q // 2) + chunk // 2) * per + c % per] = part.astype(bf16)

    core = lax.rem(x, 2)
    deep = C // 2
    pieces = Q // 2
    send(send5.at[pl.ds((1 - core) * deep, deep)], pair, 5, s, x + 1 - 2 * core)
    pending.append(lambda: sent(pair, 5))
    wait_for(pair, recv_sem.at[5])
    for i in range(pieces):
        own = send5[pl.ds(core * deep + i * per, per)].astype(f32)
        summed[i] = (own + pair[i * per : i * per + per].astype(f32)).astype(bf16)
    slot = lax.div(x, 2)

    def to_peer(i):
        to = lax.rem(lax.div(q, 2) + pieces // 2 + swing(lax.rem(i, pieces)) + pieces, pieces)
        send(summed.at[to], recv5.at[slot], 4, s, jnp.where(i < pieces, Q - side, side) + 2 * to + core)

    each(Q - 1, to_peer)
    pending.append(lambda: sent(recv5.at[pl.ds(0, Q - 1)], 4))
    keep(summed.at[lax.div(q, 2)], recv5.at[slot], 4)
    wait_for(recv5, recv_sem.at[4])
    part = recv5[0].astype(f32)
    for i in range(1, Q):
        part = part + recv5[i].astype(f32)
    recv7[q] = part.astype(bf16)
    each(Q - 1, lambda i: send(recv7.at[q], recv7.at[q], 6, s, side + lax.rem(q + Q // 2 + swing(i) + Q, Q)))
    pending.append(lambda: sent(recv7.at[pl.ds(0, Q - 1)], 6))
    loads[5].wait()
    wait_for(recv7.at[pl.ds(0, Q - 1)], recv_sem.at[6])

    wide = jnp.concatenate([recv7[c // per, c % per] for c in range(C)], axis=1)
    term = dot(wide, tokens[...].reshape(wide.shape[1], 128), 1, 0)
    term8[...] = term.astype(bf16)

    def to_plane(i):
        to = far_end(i)

        @pl.when(to != s)
        def _():
            send(term8, recv8.at[s], 7, to, x)

        @pl.when(to == s)
        def _():
            keep(term8, recv8.at[s], 7)

    each(S, to_plane)

    for c in range(C):
        left = jnp.concatenate([disp[c].astype(bf16), recv7[c // per, c % per]], axis=0)
        right = jnp.concatenate([backs[c], params[...]], axis=0)
        gtok[c] = dot(left, right, 0, 0).astype(bf16)
    store_tok = pltpu.make_async_copy(gtok, gtok_h, out_sem.at[2])
    store_tok.start()

    for wait in pending:
        wait()
    store_out.wait()
    store_in.wait()
    store_tok.wait()
    wait_for(recv8, recv_sem.at[7])
    sent(recv8.at[pl.ds(0, S - 1)], 7)


def hand_over(terms_h, a_h, b_h, c_h, to_slot, to_a, to_b, to_c, terms, a, b, c, slot, sem):
    sources, held, targets = (terms_h, a_h, b_h, c_h), (terms, a, b, c), (to_slot, to_a, to_b, to_c)
    ins = [pltpu.make_async_copy(sources[i], held[i], sem.at[i]) for i in range(4)]
    outs = [pltpu.make_async_copy((slot, a, b, c)[i], targets[i], sem.at[4 + i]) for i in range(4)]
    for copy in ins:
        copy.start()
    for i in range(1, 4):
        ins[i].wait()
        outs[i].start()
    ins[0].wait()
    sums = [terms[i].astype(f32) for i in range(4)]
    for i in range(4, terms.shape[0]):
        sums[i % 4] = sums[i % 4] + terms[i].astype(f32)
    slot[...] = (sums[0] + sums[1]) + (sums[2] + sums[3])
    outs[0].start()
    for copy in outs:
        copy.wait()


def solution(mesh):
    S, E = mesh.shape["seq"], mesh.shape["exp"]

    def body(tokens, grad_out, logits, slot_params, weight_in, weight_out):
        C, M, D = tokens.shape
        _, wide, F = weight_in.shape
        args = (tokens, grad_out, logits, slot_params, weight_in[0], weight_out[0])
        outs = (
            jax.ShapeDtypeStruct((C, M, D), bf16),
            jax.ShapeDtypeStruct((E, D), f32),
            jax.ShapeDtypeStruct((wide, F), bf16),
            jax.ShapeDtypeStruct((F, wide), bf16),
        )
        Q = E // 2
        per = C // Q
        hold = lambda a: pltpu.VMEM(a.shape, a.dtype)
        terms = jax.ShapeDtypeStruct((S, E, D), bf16)
        term = jax.ShapeDtypeStruct((E, D), bf16)
        scratch = (
            [hold(a) for a in args]
            + [hold(a) for a in (outs[0], term, outs[2], outs[3])]
            + [
                pltpu.VMEM((C, E, M), f32),
                pltpu.VMEM((C, E, M), f32),
                pltpu.VMEM((E, 16, D), bf16),
                pltpu.VMEM((S, 16, D), bf16),
                pltpu.VMEM((16, D), bf16),
                pltpu.VMEM((E, 16, D), bf16),
                pltpu.VMEM((E, 16, D), bf16),
                pltpu.VMEM((S, 16, D), bf16),
                pltpu.VMEM((16, D), bf16),
                pltpu.VMEM((E, 16, D), bf16),
                pltpu.VMEM((1, 128), f32),
                pltpu.VMEM((S, 128), f32),
                pltpu.VMEM((1, 128), f32),
                pltpu.VMEM((E, 128), f32),
                pltpu.VMEM((128, S), f32),
                pltpu.VMEM((C, E, M), bf16),
                pltpu.VMEM((C // 2, E, M), bf16),
                pltpu.VMEM((Q // 2, per, E, M), bf16),
                pltpu.VMEM((Q, per, E, M), bf16),
                pltpu.VMEM((Q, per, E, M), bf16),
                pltpu.VMEM((8, D), f32),
                pltpu.VMEM((8, D), f32),
                pltpu.SemaphoreType.DMA((6,)),
                pltpu.SemaphoreType.DMA((4,)),
                pltpu.SemaphoreType.DMA((10,)),
                pltpu.SemaphoreType.DMA((10,)),
                pltpu.SemaphoreType.REGULAR,
            ]
        )
        gtok, parts, gwin, gwout = pl.pallas_call(
            functools.partial(kernel, S, E, C),
            out_shape=(outs[0], terms, outs[2], outs[3]),
            in_specs=[pl.BlockSpec(memory_space=pltpu.HBM)] * 6,
            out_specs=[pl.BlockSpec(memory_space=pl.ANY)] * 4,
            scratch_shapes=scratch,
            compiler_params=pltpu.CompilerParams(
                collective_id=0, has_side_effects=True, vmem_limit_bytes=60 << 20
            ),
            name="moe_backward",
        )(*args)
        gslot, gtok, gwin, gwout = pl.pallas_call(
            hand_over,
            out_shape=(outs[1], outs[0], outs[2], outs[3]),
            in_specs=[pl.BlockSpec(memory_space=pl.ANY)] * 4,
            out_specs=[pl.BlockSpec(memory_space=pltpu.HBM)] * 4,
            scratch_shapes=[hold(a) for a in (terms, outs[0], outs[2], outs[3], outs[1])]
            + [pltpu.SemaphoreType.DMA((8,))],
            name="hand_over",
        )(parts, gtok, gwin, gwout)
        return gtok, gslot, gwin[None], gwout[None]

    in_specs = (
        P(None, "seq", "exp"),
        P(None, "seq", "exp"),
        P(None, None, "seq"),
        P(None, "exp"),
        P("exp", None, "seq"),
        P("exp", "seq", None),
    )
    out_specs = (
        P(None, "seq", "exp"),
        P(None, "exp"),
        P("exp", None, "seq"),
        P("exp", "seq", None),
    )
    return jax.shard_map(body, mesh=mesh, in_specs=in_specs, out_specs=out_specs, check_vma=False)
```

```python
import functools

import jax
import jax.numpy as jnp
from jax import lax
from jax.experimental import pallas as pl
from jax.experimental.pallas import tpu as pltpu
from jax.sharding import PartitionSpec as P

root_coef = 0.7978845608028654
cubic_coef = 0.044715
MESH = pl.DeviceIdType.MESH
f32 = jnp.float32
bf16 = jnp.bfloat16
LINE = 8


def gelu_parts(pre_act):
    tanh_value = jnp.tanh(root_coef * (pre_act + cubic_coef * pre_act * pre_act * pre_act))
    activated = 0.5 * pre_act * (1.0 + tanh_value)
    derivative = 0.5 * (1.0 + tanh_value) + 0.5 * pre_act * (
        1.0 - tanh_value * tanh_value
    ) * root_coef * (1.0 + 3.0 * cubic_coef * pre_act * pre_act)
    return (activated, derivative)


def dot(a, b, ca, cb):
    return lax.dot_general(a, b, (((ca,), (cb,)), ((), ())), preferred_element_type=f32)


def wait_for(ref, sem):
    pltpu.make_async_copy(ref, ref, sem).wait()


def each(count, step):
    def run(i, carry):
        step(i)
        return carry

    lax.fori_loop(0, count, run, 0)


def kernel(
    S, E, C,
    tokens_h, grad_h, logits_h, params_h, win_h, wout_h,
    gtok_h, recv8, gwin_h, gwout_h,
    tokens, grad, logits, params, win, wout,
    gtok, term8, gwin, gwout,
    comb, disp,
    send1, recv1, send2, rows, send3, recv3, send4, recv4,
    row1, rows1, row4, rows4, turned,
    send5, pair, summed, recv5, recv7,
    slot_keep, lse_keep,
    in_sem, out_sem, send_sem, recv_sem, go_sem,
):
    s = lax.axis_index("seq")
    x = lax.axis_index("exp")
    half = LINE // 2
    Q = E // 2
    per = C // Q
    q = lax.rem(x, Q)
    side = x - q
    across = lax.rem(x + Q, E)

    def owner(e):
        return lax.div(e, half) * LINE + LINE // 4 + lax.rem(e, half)

    z = lax.rem(s, LINE)
    lines = S // LINE

    def swing(i):
        return jnp.where(lax.rem(i, 2) == 1, lax.div(i + 1, 2), -lax.div(i + 1, 2))

    def far_line(i):
        return lax.rem(lax.div(s, LINE) + lines // 2 + swing(lax.rem(i, lines)) + lines, lines)

    def far_ring(i, start):
        return far_line(i) * LINE + lax.rem(z + start + swing(lax.div(i, lines)) + LINE, LINE)

    def far_end(i):
        k = lax.div(i, lines)
        return far_line(i) * LINE + jnp.where(z < half, LINE - 1 - k, k)

    is_owner = jnp.logical_and(z >= LINE // 4, z < LINE // 4 + half)
    mine = lax.div(s, LINE) * half + jnp.clip(z - LINE // 4, 0, half - 1)
    both = jnp.logical_and(is_owner, mine == x)
    home = owner(x)

    barrier = pltpu.get_barrier_semaphore()

    def greet(ds, dx):
        pl.semaphore_signal(barrier, inc=1, device_id=(ds, dx), device_id_type=MESH)

    @pl.when(is_owner)
    def _():
        def to_rest(i):
            k = lax.rem(i + s, S - E)
            zz = lax.rem(k, half)
            greet(lax.div(k, half) * LINE + jnp.where(zz < LINE // 4, zz, zz + half), x)

        each(S - E, to_rest)

    def to_far(i):
        to = lax.rem(x + Q + i, E)

        @pl.when(jnp.logical_or(jnp.logical_not(both), to != x))
        def _():
            greet(home, to)

    each(E, to_far)

    loads = []
    for i, (a, b) in enumerate(
        ((logits_h, logits), (tokens_h, tokens), (grad_h, grad), (win_h, win), (wout_h, wout), (params_h, params))
    ):
        copy = pltpu.make_async_copy(a, b, in_sem.at[i])
        copy.start()
        loads.append(copy)

    def send(src, dst, k, ds, dx):
        pltpu.make_async_remote_copy(
            src_ref=src, dst_ref=dst, send_sem=send_sem.at[k], recv_sem=recv_sem.at[k],
            device_id=(ds, dx), device_id_type=MESH,
        ).start()

    def keep(src, dst, k):
        pltpu.make_async_copy(src, dst, recv_sem.at[k]).start()

    pending = []

    def sent(ref, k):
        wait_for(ref, send_sem.at[k])

    def diagonal(count, shift):
        down = lax.broadcasted_iota(jnp.int32, (count, 128), 0)
        along = lax.broadcasted_iota(jnp.int32, (count, 128), 1)
        return along == down + shift

    loads[0].wait()
    loads[1].wait()
    loads[2].wait()
    slot_parts, grad_parts, lse_parts = [], [], []
    for c in range(C):
        value = logits[c]
        top = jnp.max(value, axis=1, keepdims=True)
        weight = jnp.exp(value - top)
        mass = jnp.sum(weight, axis=1, keepdims=True)
        slot_parts.append(dot((weight / mass).astype(bf16), tokens[c], 1, 0))
        lse_parts.append(jnp.broadcast_to(top + jnp.log(mass), (E, 128)))
        crest = jnp.max(value, axis=0, keepdims=True)
        share = jnp.exp(value - crest)
        share = share / jnp.sum(share, axis=0, keepdims=True)
        comb[c] = share
        grad_parts.append(dot(share.astype(bf16), grad[c], 1, 0))
    send1[...] = jnp.concatenate(
        [jnp.swapaxes(jnp.stack(slot_parts), 0, 1), jnp.swapaxes(jnp.stack(grad_parts), 0, 1)], axis=1
    ).astype(bf16)
    spread = jnp.swapaxes(jnp.stack(lse_parts), 0, 1).reshape(E * 8, 128)
    row1[...] = jnp.sum(jnp.where(diagonal(E * 8, 0), spread, 0.0), axis=0, keepdims=True)

    @pl.when(jnp.logical_not(is_owner))
    def _():
        pl.semaphore_wait(barrier, E)

        def go(first):
            for i in range(half // 2):
                to = s - z + first + i
                pl.semaphore_signal(go_sem, inc=1, device_id=(to, x), device_id_type=MESH)

        @pl.when(z == LINE // 4 - 1)
        def _():
            go(LINE // 4)

        @pl.when(z == LINE // 4 + half)
        def _():
            go(LINE // 4 + half // 2)

    @pl.when(is_owner)
    def _():
        pl.semaphore_wait(go_sem, 1)

    def to_owner(i):
        k = lax.div(i, lines)
        e = far_line(i) * half + jnp.where(z < half, half - 1 - k, k)
        to = owner(e)

        @pl.when(to != s)
        def _():
            send(row1, rows1.at[pl.ds(s, 1)], 8, to, x)
            send(send1.at[e], recv1.at[s], 0, to, x)

        @pl.when(to == s)
        def _():
            keep(row1, rows1.at[pl.ds(s, 1)], 8)
            keep(send1.at[e], recv1.at[s], 0)

    each(E, to_owner)

    def sent_first():
        sent(send1.at[pl.ds(0, E - 1)], 0)
        each(E - 1, lambda i: sent(row1, 8))

        @pl.when(jnp.logical_not(is_owner))
        def _():
            sent(send1.at[0], 0)
            sent(row1, 8)

    pending.append(sent_first)

    @pl.when(is_owner)
    def _():
        wait_for(rows1, recv_sem.at[8])
        turned[...] = jnp.transpose(rows1[...])
        lses = turned[pl.ds(pl.multiple_of(mine * 8, 8), 8), :]
        top = jnp.max(lses, axis=1, keepdims=True)
        weights = jnp.exp(lses - top)
        total = jnp.sum(weights, axis=1, keepdims=True)
        weights = weights / total
        lse_keep[...] = jnp.broadcast_to(top + jnp.log(total), (8, 128))
        wait_for(recv1, recv_sem.at[0])
        slots = jnp.zeros((8, 128), f32)
        grads = jnp.zeros((8, 128), f32)
        for i in range(S):
            piece = recv1[i].astype(f32)
            slots = slots + weights[:, i : i + 1] * piece[0:8]
            grads = grads + piece[8:16]
        slot_keep[...] = slots
        send2[...] = jnp.concatenate([slots, grads], axis=0).astype(bf16)

        pl.semaphore_wait(barrier, S - both.astype(jnp.int32))
        start = jnp.where(lax.div(mine, Q) == lax.div(x, Q), half, 0)

        def to_expert(i):
            to = far_ring(i, start)
            own = jnp.logical_and(both, to == s)

            @pl.when(jnp.logical_not(own))
            def _():
                send(send2, rows.at[x], 1, to, mine)

            @pl.when(own)
            def _():
                keep(send2, rows.at[x], 1)

        each(S, to_expert)

    def sent_rows():
        @pl.when(is_owner)
        def _():
            each(S - 1, lambda i: sent(send2, 1))

            @pl.when(jnp.logical_not(both))
            def _():
                sent(send2, 1)

    pending.append(sent_rows)
    loads[3].wait()
    loads[4].wait()
    wait_for(rows, recv_sem.at[1])
    held = jnp.concatenate([rows[i] for i in range(E)], axis=1)
    pre_act = dot(held, win[...], 1, 0)
    act_grad = dot(held, wout[...], 1, 1)
    activated, derivative = gelu_parts(pre_act[0:8])
    pre_grad = act_grad[8:16] * derivative
    stacked = jnp.concatenate([activated, pre_grad], axis=0).astype(bf16)
    out_part = dot(stacked, wout[...], 1, 0)
    back_part = dot(stacked, win[...], 1, 1)
    for i in range(E):
        cut = slice(i * 128, i * 128 + 128)
        send3[i] = jnp.concatenate([out_part[0:8, cut], back_part[8:16, cut]], axis=0).astype(bf16)

    def to_home(i):
        to = jnp.where(i < Q, Q - side, side) + lax.rem(q + Q // 2 + swing(lax.rem(i, Q)) + Q, Q)
        own = jnp.logical_and(both, to == x)

        @pl.when(jnp.logical_not(own))
        def _():
            send(send3.at[to], recv3.at[s], 2, home, to)

        @pl.when(own)
        def _():
            keep(send3.at[to], recv3.at[s], 2)

    each(E, to_home)

    def sent_parts():
        sent(send3.at[pl.ds(0, E - 1)], 2)

        @pl.when(jnp.logical_not(both))
        def _():
            sent(send3.at[0], 2)

    pending.append(sent_parts)

    blank = jnp.zeros((8, 128), f32)
    gwout[...] = dot(jnp.concatenate([blank, activated], axis=0).astype(bf16), held, 0, 0).astype(bf16)
    gwin[...] = dot(held, jnp.concatenate([pre_grad, blank], axis=0).astype(bf16), 0, 0).astype(bf16)
    store_out = pltpu.make_async_copy(gwout, gwout_h, out_sem.at[0])
    store_in = pltpu.make_async_copy(gwin, gwin_h, out_sem.at[1])
    store_out.start()
    store_in.start()

    @pl.when(is_owner)
    def _():
        wait_for(recv3, recv_sem.at[2])
        sums = [recv3[i].astype(f32) for i in range(4)]
        for i in range(4, S):
            sums[i % 4] = sums[i % 4] + recv3[i].astype(f32)
        total = (sums[0] + sums[1]) + (sums[2] + sums[3])
        send4[...] = total.astype(bf16)
        stat = jnp.sum(total[8:16].astype(bf16).astype(f32) * slot_keep[...], axis=1, keepdims=True)
        row4[...] = jnp.sum(
            jnp.where(diagonal(8, 0), lse_keep[...], jnp.where(diagonal(8, 8), stat, 0.0)), axis=0, keepdims=True
        )

        def to_line(i):
            to = far_ring(i, half)
            send(row4, rows4.at[pl.ds(mine, 1)], 9, to, x)
            send(send4, recv4.at[mine], 3, to, x)

        each(S - 1, to_line)
        keep(row4, rows4.at[pl.ds(mine, 1)], 9)
        keep(send4, recv4.at[mine], 3)

    def sent_sums():
        @pl.when(is_owner)
        def _():
            each(S - 1, lambda i: sent(send4, 3))
            each(S - 1, lambda i: sent(row4, 9))

    pending.append(sent_sums)
    wait_for(recv4, recv_sem.at[3])
    wait_for(rows4, recv_sem.at[9])
    sums = recv4[...].astype(f32)
    outs = jnp.swapaxes(sums[:, 0:8, :], 0, 1).astype(bf16)
    backs = jnp.swapaxes(sums[:, 8:16, :], 0, 1).astype(bf16)
    scales = rows4[...]
    def logit_part(c):
        comb_grad = dot(outs[c], grad[c], 1, 1)
        disp_grad = dot(backs[c], tokens[c], 1, 1)
        dispatch = jnp.exp(logits[c] - scales[:, c : c + 1])
        share = comb[c]
        disp[c] = dispatch
        part = share * (
            comb_grad - jnp.sum(share * comb_grad, axis=0, keepdims=True)
        ) + dispatch * (disp_grad - scales[:, C + c : C + c + 1])
        chunk = c // per
        send5[(chunk % 2 * (Q // 2) + chunk // 2) * per + c % per] = part.astype(bf16)

    core = lax.rem(x, 2)
    deep = C // 2
    pieces = Q // 2

    for parity in range(2):
        @pl.when(core == parity)
        def _():
            for c in range(C):
                if c // per % 2 != parity:
                    logit_part(c)
            send(send5.at[pl.ds((1 - parity) * deep, deep)], pair, 5, s, x + 1 - 2 * parity)
            for c in range(C):
                if c // per % 2 == parity:
                    logit_part(c)

    pending.append(lambda: sent(pair, 5))
    wait_for(pair, recv_sem.at[5])
    for i in range(pieces):
        own = send5[pl.ds(core * deep + i * per, per)].astype(f32)
        summed[i] = (own + pair[i * per : i * per + per].astype(f32)).astype(bf16)
    slot = lax.div(x, 2)

    def to_peer(i):
        to = lax.rem(lax.div(q, 2) + pieces // 2 + swing(lax.rem(i, pieces)) + pieces, pieces)
        send(summed.at[to], recv5.at[slot], 4, s, jnp.where(i < pieces, Q - side, side) + 2 * to + core)

    each(Q - 1, to_peer)
    pending.append(lambda: sent(recv5.at[pl.ds(0, Q - 1)], 4))
    keep(summed.at[lax.div(q, 2)], recv5.at[slot], 4)
    wait_for(recv5, recv_sem.at[4])
    part = recv5[0].astype(f32)
    for i in range(1, Q):
        part = part + recv5[i].astype(f32)
    recv7[q] = part.astype(bf16)
    each(Q - 1, lambda i: send(recv7.at[q], recv7.at[q], 6, s, side + lax.rem(q + Q // 2 + swing(i) + Q, Q)))
    pending.append(lambda: sent(recv7.at[pl.ds(0, Q - 1)], 6))
    loads[5].wait()
    wait_for(recv7.at[pl.ds(0, Q - 1)], recv_sem.at[6])

    wide = jnp.concatenate([recv7[c // per, c % per] for c in range(C)], axis=1)
    term = dot(wide, tokens[...].reshape(wide.shape[1], 128), 1, 0)
    term8[...] = term.astype(bf16)

    def to_plane(i):
        to = far_end(i)

        @pl.when(to != s)
        def _():
            send(term8, recv8.at[s], 7, to, x)

        @pl.when(to == s)
        def _():
            keep(term8, recv8.at[s], 7)

    each(S, to_plane)

    for c in range(C):
        left = jnp.concatenate([disp[c].astype(bf16), recv7[c // per, c % per]], axis=0)
        right = jnp.concatenate([backs[c], params[...]], axis=0)
        gtok[c] = dot(left, right, 0, 0).astype(bf16)
    store_tok = pltpu.make_async_copy(gtok, gtok_h, out_sem.at[2])
    store_tok.start()

    for wait in pending:
        wait()
    store_out.wait()
    store_in.wait()
    store_tok.wait()
    wait_for(recv8, recv_sem.at[7])
    sent(recv8.at[pl.ds(0, S - 1)], 7)


def hand_over(terms_h, a_h, b_h, c_h, to_slot, to_a, to_b, to_c, terms, a, b, c, slot, sem):
    sources, held, targets = (terms_h, a_h, b_h, c_h), (terms, a, b, c), (to_slot, to_a, to_b, to_c)
    ins = [pltpu.make_async_copy(sources[i], held[i], sem.at[i]) for i in range(4)]
    outs = [pltpu.make_async_copy((slot, a, b, c)[i], targets[i], sem.at[4 + i]) for i in range(4)]
    for copy in ins:
        copy.start()
    for i in range(1, 4):
        ins[i].wait()
        outs[i].start()
    ins[0].wait()
    sums = [terms[i].astype(f32) for i in range(4)]
    for i in range(4, terms.shape[0]):
        sums[i % 4] = sums[i % 4] + terms[i].astype(f32)
    slot[...] = (sums[0] + sums[1]) + (sums[2] + sums[3])
    outs[0].start()
    for copy in outs:
        copy.wait()


def solution(mesh):
    S, E = mesh.shape["seq"], mesh.shape["exp"]

    def body(tokens, grad_out, logits, slot_params, weight_in, weight_out):
        C, M, D = tokens.shape
        _, wide, F = weight_in.shape
        args = (tokens, grad_out, logits, slot_params, weight_in[0], weight_out[0])
        outs = (
            jax.ShapeDtypeStruct((C, M, D), bf16),
            jax.ShapeDtypeStruct((E, D), f32),
            jax.ShapeDtypeStruct((wide, F), bf16),
            jax.ShapeDtypeStruct((F, wide), bf16),
        )
        Q = E // 2
        per = C // Q
        hold = lambda a: pltpu.VMEM(a.shape, a.dtype)
        terms = jax.ShapeDtypeStruct((S, E, D), bf16)
        term = jax.ShapeDtypeStruct((E, D), bf16)
        scratch = (
            [hold(a) for a in args]
            + [hold(a) for a in (outs[0], term, outs[2], outs[3])]
            + [
                pltpu.VMEM((C, E, M), f32),
                pltpu.VMEM((C, E, M), f32),
                pltpu.VMEM((E, 16, D), bf16),
                pltpu.VMEM((S, 16, D), bf16),
                pltpu.VMEM((16, D), bf16),
                pltpu.VMEM((E, 16, D), bf16),
                pltpu.VMEM((E, 16, D), bf16),
                pltpu.VMEM((S, 16, D), bf16),
                pltpu.VMEM((16, D), bf16),
                pltpu.VMEM((E, 16, D), bf16),
                pltpu.VMEM((1, 128), f32),
                pltpu.VMEM((S, 128), f32),
                pltpu.VMEM((1, 128), f32),
                pltpu.VMEM((E, 128), f32),
                pltpu.VMEM((128, S), f32),
                pltpu.VMEM((C, E, M), bf16),
                pltpu.VMEM((C // 2, E, M), bf16),
                pltpu.VMEM((Q // 2, per, E, M), bf16),
                pltpu.VMEM((Q, per, E, M), bf16),
                pltpu.VMEM((Q, per, E, M), bf16),
                pltpu.VMEM((8, D), f32),
                pltpu.VMEM((8, D), f32),
                pltpu.SemaphoreType.DMA((6,)),
                pltpu.SemaphoreType.DMA((4,)),
                pltpu.SemaphoreType.DMA((10,)),
                pltpu.SemaphoreType.DMA((10,)),
                pltpu.SemaphoreType.REGULAR,
            ]
        )
        gtok, parts, gwin, gwout = pl.pallas_call(
            functools.partial(kernel, S, E, C),
            out_shape=(outs[0], terms, outs[2], outs[3]),
            in_specs=[pl.BlockSpec(memory_space=pltpu.HBM)] * 6,
            out_specs=[pl.BlockSpec(memory_space=pl.ANY)] * 4,
            scratch_shapes=scratch,
            compiler_params=pltpu.CompilerParams(
                collective_id=0, has_side_effects=True, vmem_limit_bytes=60 << 20
            ),
            name="moe_backward",
        )(*args)
        gslot, gtok, gwin, gwout = pl.pallas_call(
            hand_over,
            out_shape=(outs[1], outs[0], outs[2], outs[3]),
            in_specs=[pl.BlockSpec(memory_space=pl.ANY)] * 4,
            out_specs=[pl.BlockSpec(memory_space=pltpu.HBM)] * 4,
            scratch_shapes=[hold(a) for a in (terms, outs[0], outs[2], outs[3], outs[1])]
            + [pltpu.SemaphoreType.DMA((8,))],
            name="hand_over",
        )(parts, gtok, gwin, gwout)
        return gtok, gslot, gwin[None], gwout[None]

    in_specs = (
        P(None, "seq", "exp"),
        P(None, "seq", "exp"),
        P(None, None, "seq"),
        P(None, "exp"),
        P("exp", None, "seq"),
        P("exp", "seq", None),
    )
    out_specs = (
        P(None, "seq", "exp"),
        P(None, "exp"),
        P("exp", None, "seq"),
        P("exp", "seq", None),
    )
    return jax.shard_map(body, mesh=mesh, in_specs=in_specs, out_specs=out_specs, check_vma=False)
```

```python
import functools

import jax
import jax.numpy as jnp
from jax import lax
from jax.experimental import pallas as pl
from jax.experimental.pallas import tpu as pltpu
from jax.sharding import PartitionSpec as P

root_coef = 0.7978845608028654
cubic_coef = 0.044715
MESH = pl.DeviceIdType.MESH
f32 = jnp.float32
bf16 = jnp.bfloat16
LINE = 8


def gelu_parts(pre_act):
    tanh_value = jnp.tanh(root_coef * (pre_act + cubic_coef * pre_act * pre_act * pre_act))
    activated = 0.5 * pre_act * (1.0 + tanh_value)
    derivative = 0.5 * (1.0 + tanh_value) + 0.5 * pre_act * (
        1.0 - tanh_value * tanh_value
    ) * root_coef * (1.0 + 3.0 * cubic_coef * pre_act * pre_act)
    return (activated, derivative)


def dot(a, b, ca, cb):
    return lax.dot_general(a, b, (((ca,), (cb,)), ((), ())), preferred_element_type=f32)


def wait_for(ref, sem):
    pltpu.make_async_copy(ref, ref, sem).wait()


def each(count, step):
    def run(i, carry):
        step(i)
        return carry

    lax.fori_loop(0, count, run, 0)


def kernel(
    S, E, C,
    tokens_h, grad_h, logits_h, params_h, win_h, wout_h,
    gtok_h, recv8, gwin_h, gwout_h,
    tokens, grad, logits, params, win, wout,
    gtok, term8, gwin, gwout,
    comb, disp,
    send1, recv1, send2, rows, send3, recv3, send4, recv4,
    row1, rows1, row4, rows4, turned,
    send5, pair, summed, recv5, recv7,
    slot_keep, lse_keep,
    in_sem, out_sem, send_sem, recv_sem, go_sem,
):
    s = lax.axis_index("seq")
    x = lax.axis_index("exp")
    half = LINE // 2
    Q = E // 2
    per = C // Q
    q = lax.rem(x, Q)
    side = x - q
    across = lax.rem(x + Q, E)

    def owner(e):
        return lax.div(e, half) * LINE + LINE // 4 + lax.rem(e, half)

    z = lax.rem(s, LINE)
    lines = S // LINE

    def swing(i):
        return jnp.where(lax.rem(i, 2) == 1, lax.div(i + 1, 2), -lax.div(i + 1, 2))

    def far_line(i):
        return lax.rem(lax.div(s, LINE) + lines // 2 + swing(lax.rem(i, lines)) + lines, lines)

    def far_ring(i, start):
        return far_line(i) * LINE + lax.rem(z + start + swing(lax.div(i, lines)) + LINE, LINE)

    def far_end(i):
        k = lax.div(i, lines)
        return far_line(i) * LINE + jnp.where(z < half, LINE - 1 - k, k)

    is_owner = jnp.logical_and(z >= LINE // 4, z < LINE // 4 + half)
    mine = lax.div(s, LINE) * half + jnp.clip(z - LINE // 4, 0, half - 1)
    both = jnp.logical_and(is_owner, mine == x)
    home = owner(x)

    barrier = pltpu.get_barrier_semaphore()

    def greet(ds, dx):
        pl.semaphore_signal(barrier, inc=1, device_id=(ds, dx), device_id_type=MESH)

    @pl.when(is_owner)
    def _():
        def to_rest(i):
            k = lax.rem(i + s, S - E)
            zz = lax.rem(k, half)
            greet(lax.div(k, half) * LINE + jnp.where(zz < LINE // 4, zz, zz + half), x)

        each(S - E, to_rest)

    def to_far(i):
        to = lax.rem(x + Q + i, E)

        @pl.when(jnp.logical_or(jnp.logical_not(both), to != x))
        def _():
            greet(home, to)

    each(E, to_far)

    loads = []
    for i, (a, b) in enumerate(
        ((logits_h, logits), (tokens_h, tokens), (grad_h, grad), (win_h, win), (wout_h, wout), (params_h, params))
    ):
        copy = pltpu.make_async_copy(a, b, in_sem.at[i])
        copy.start()
        loads.append(copy)

    def send(src, dst, k, ds, dx):
        pltpu.make_async_remote_copy(
            src_ref=src, dst_ref=dst, send_sem=send_sem.at[k], recv_sem=recv_sem.at[k],
            device_id=(ds, dx), device_id_type=MESH,
        ).start()

    def keep(src, dst, k):
        pltpu.make_async_copy(src, dst, recv_sem.at[k]).start()

    pending = []

    def sent(ref, k):
        wait_for(ref, send_sem.at[k])

    def diagonal(count, shift):
        down = lax.broadcasted_iota(jnp.int32, (count, 128), 0)
        along = lax.broadcasted_iota(jnp.int32, (count, 128), 1)
        return along == down + shift

    loads[0].wait()
    loads[1].wait()
    loads[2].wait()
    slot_parts, grad_parts, lse_parts = [], [], []
    for c in range(C):
        value = logits[c]
        top = jnp.max(value, axis=1, keepdims=True)
        weight = jnp.exp(value - top)
        mass = jnp.sum(weight, axis=1, keepdims=True)
        slot_parts.append(dot((weight / mass).astype(bf16), tokens[c], 1, 0))
        lse_parts.append(jnp.broadcast_to(top + jnp.log(mass), (E, 128)))
        crest = jnp.max(value, axis=0, keepdims=True)
        share = jnp.exp(value - crest)
        share = share / jnp.sum(share, axis=0, keepdims=True)
        comb[c] = share
        grad_parts.append(dot(share.astype(bf16), grad[c], 1, 0))
    send1[...] = jnp.concatenate(
        [jnp.swapaxes(jnp.stack(slot_parts), 0, 1), jnp.swapaxes(jnp.stack(grad_parts), 0, 1)], axis=1
    ).astype(bf16)
    spread = jnp.swapaxes(jnp.stack(lse_parts), 0, 1).reshape(E * 8, 128)
    row1[...] = jnp.sum(jnp.where(diagonal(E * 8, 0), spread, 0.0), axis=0, keepdims=True)

    @pl.when(jnp.logical_not(is_owner))
    def _():
        pl.semaphore_wait(barrier, E)

        def go(first):
            for i in range(half // 2):
                to = s - z + first + i
                pl.semaphore_signal(go_sem, inc=1, device_id=(to, x), device_id_type=MESH)

        @pl.when(z == LINE // 4 - 1)
        def _():
            go(LINE // 4)

        @pl.when(z == LINE // 4 + half)
        def _():
            go(LINE // 4 + half // 2)

    @pl.when(is_owner)
    def _():
        pl.semaphore_wait(go_sem, 1)

    def to_owner(i):
        k = lax.div(i, lines)
        e = far_line(i) * half + jnp.where(z < half, half - 1 - k, k)
        to = owner(e)

        @pl.when(to != s)
        def _():
            send(row1, rows1.at[pl.ds(s, 1)], 8, to, x)
            send(send1.at[e], recv1.at[s], 0, to, x)

        @pl.when(to == s)
        def _():
            keep(row1, rows1.at[pl.ds(s, 1)], 8)
            keep(send1.at[e], recv1.at[s], 0)

    each(E, to_owner)

    def sent_first():
        sent(send1.at[pl.ds(0, E - 1)], 0)
        each(E - 1, lambda i: sent(row1, 8))

        @pl.when(jnp.logical_not(is_owner))
        def _():
            sent(send1.at[0], 0)
            sent(row1, 8)

    pending.append(sent_first)

    @pl.when(is_owner)
    def _():
        wait_for(rows1, recv_sem.at[8])
        turned[...] = jnp.transpose(rows1[...])
        lses = turned[pl.ds(pl.multiple_of(mine * 8, 8), 8), :]
        top = jnp.max(lses, axis=1, keepdims=True)
        weights = jnp.exp(lses - top)
        total = jnp.sum(weights, axis=1, keepdims=True)
        weights = weights / total
        lse_keep[...] = jnp.broadcast_to(top + jnp.log(total), (8, 128))
        wait_for(recv1, recv_sem.at[0])
        slots = jnp.zeros((8, 128), f32)
        grads = jnp.zeros((8, 128), f32)
        for i in range(S):
            piece = recv1[i].astype(f32)
            slots = slots + weights[:, i : i + 1] * piece[0:8]
            grads = grads + piece[8:16]
        slot_keep[...] = slots
        send2[...] = jnp.concatenate([slots, grads], axis=0).astype(bf16)

        pl.semaphore_wait(barrier, S - both.astype(jnp.int32))
        start = jnp.where(lax.div(mine, Q) == lax.div(x, Q), half, 0)

        def to_expert(i):
            to = far_ring(i, start)
            own = jnp.logical_and(both, to == s)

            @pl.when(jnp.logical_not(own))
            def _():
                send(send2, rows.at[x], 1, to, mine)

            @pl.when(own)
            def _():
                keep(send2, rows.at[x], 1)

        each(S, to_expert)

    def sent_rows():
        @pl.when(is_owner)
        def _():
            each(S - 1, lambda i: sent(send2, 1))

            @pl.when(jnp.logical_not(both))
            def _():
                sent(send2, 1)

    pending.append(sent_rows)
    loads[3].wait()
    loads[4].wait()
    wait_for(rows, recv_sem.at[1])
    held = jnp.concatenate([rows[i] for i in range(E)], axis=1)
    pre_act = dot(held, win[...], 1, 0)
    act_grad = dot(held, wout[...], 1, 1)
    activated, derivative = gelu_parts(pre_act[0:8])
    pre_grad = act_grad[8:16] * derivative
    stacked = jnp.concatenate([activated, pre_grad], axis=0).astype(bf16)
    def to_home(i):
        to = jnp.where(i < Q, Q - side, side) + lax.rem(q + Q // 2 + swing(lax.rem(i, Q)) + Q, Q)
        own = jnp.logical_and(both, to == x)

        @pl.when(jnp.logical_not(own))
        def _():
            send(send3.at[to], recv3.at[s], 2, home, to)

        @pl.when(own)
        def _():
            keep(send3.at[to], recv3.at[s], 2)

    for turn in range(2):
        base = side if turn else Q - side
        cut = pl.ds(pl.multiple_of(base * 128, 128), Q * 128)
        out_part = dot(stacked, wout[:, cut], 1, 0)
        back_part = dot(stacked, win[cut, :], 1, 1)
        for i in range(Q):
            lanes = slice(i * 128, i * 128 + 128)
            send3[base + i] = jnp.concatenate([out_part[0:8, lanes], back_part[8:16, lanes]], axis=0).astype(bf16)
        each(Q, lambda i: to_home(i + turn * Q))

    def sent_parts():
        sent(send3.at[pl.ds(0, E - 1)], 2)

        @pl.when(jnp.logical_not(both))
        def _():
            sent(send3.at[0], 2)

    pending.append(sent_parts)

    blank = jnp.zeros((8, 128), f32)
    gwout[...] = dot(jnp.concatenate([blank, activated], axis=0).astype(bf16), held, 0, 0).astype(bf16)
    gwin[...] = dot(held, jnp.concatenate([pre_grad, blank], axis=0).astype(bf16), 0, 0).astype(bf16)
    store_out = pltpu.make_async_copy(gwout, gwout_h, out_sem.at[0])
    store_in = pltpu.make_async_copy(gwin, gwin_h, out_sem.at[1])
    store_out.start()
    store_in.start()

    @pl.when(is_owner)
    def _():
        wait_for(recv3, recv_sem.at[2])
        sums = [recv3[i].astype(f32) for i in range(4)]
        for i in range(4, S):
            sums[i % 4] = sums[i % 4] + recv3[i].astype(f32)
        total = (sums[0] + sums[1]) + (sums[2] + sums[3])
        send4[...] = total.astype(bf16)
        stat = jnp.sum(total[8:16].astype(bf16).astype(f32) * slot_keep[...], axis=1, keepdims=True)
        row4[...] = jnp.sum(
            jnp.where(diagonal(8, 0), lse_keep[...], jnp.where(diagonal(8, 8), stat, 0.0)), axis=0, keepdims=True
        )

        def to_line(i):
            to = far_ring(i, half)
            send(row4, rows4.at[pl.ds(mine, 1)], 9, to, x)
            send(send4, recv4.at[mine], 3, to, x)

        each(S - 1, to_line)
        keep(row4, rows4.at[pl.ds(mine, 1)], 9)
        keep(send4, recv4.at[mine], 3)

    def sent_sums():
        @pl.when(is_owner)
        def _():
            each(S - 1, lambda i: sent(send4, 3))
            each(S - 1, lambda i: sent(row4, 9))

    pending.append(sent_sums)
    wait_for(recv4, recv_sem.at[3])
    wait_for(rows4, recv_sem.at[9])
    sums = recv4[...].astype(f32)
    outs = jnp.swapaxes(sums[:, 0:8, :], 0, 1).astype(bf16)
    backs = jnp.swapaxes(sums[:, 8:16, :], 0, 1).astype(bf16)
    scales = rows4[...]
    def logit_part(c):
        comb_grad = dot(outs[c], grad[c], 1, 1)
        disp_grad = dot(backs[c], tokens[c], 1, 1)
        dispatch = jnp.exp(logits[c] - scales[:, c : c + 1])
        share = comb[c]
        disp[c] = dispatch
        part = share * (
            comb_grad - jnp.sum(share * comb_grad, axis=0, keepdims=True)
        ) + dispatch * (disp_grad - scales[:, C + c : C + c + 1])
        chunk = c // per
        send5[(chunk % 2 * (Q // 2) + chunk // 2) * per + c % per] = part.astype(bf16)

    core = lax.rem(x, 2)
    deep = C // 2
    pieces = Q // 2

    for parity in range(2):
        @pl.when(core == parity)
        def _():
            for c in range(C):
                if c // per % 2 != parity:
                    logit_part(c)
            send(send5.at[pl.ds((1 - parity) * deep, deep)], pair, 5, s, x + 1 - 2 * parity)
            for c in range(C):
                if c // per % 2 == parity:
                    logit_part(c)

    pending.append(lambda: sent(pair, 5))
    wait_for(pair, recv_sem.at[5])
    for i in range(pieces):
        own = send5[pl.ds(core * deep + i * per, per)].astype(f32)
        summed[i] = (own + pair[i * per : i * per + per].astype(f32)).astype(bf16)
    slot = lax.div(x, 2)

    def to_peer(i):
        to = lax.rem(lax.div(q, 2) + pieces // 2 + swing(lax.rem(i, pieces)) + pieces, pieces)
        send(summed.at[to], recv5.at[slot], 4, s, jnp.where(i < pieces, Q - side, side) + 2 * to + core)

    each(Q - 1, to_peer)
    pending.append(lambda: sent(recv5.at[pl.ds(0, Q - 1)], 4))
    keep(summed.at[lax.div(q, 2)], recv5.at[slot], 4)
    wait_for(recv5, recv_sem.at[4])
    part = recv5[0].astype(f32)
    for i in range(1, Q):
        part = part + recv5[i].astype(f32)
    recv7[q] = part.astype(bf16)
    each(Q - 1, lambda i: send(recv7.at[q], recv7.at[q], 6, s, side + lax.rem(q + Q // 2 + swing(i) + Q, Q)))
    pending.append(lambda: sent(recv7.at[pl.ds(0, Q - 1)], 6))
    loads[5].wait()
    wait_for(recv7.at[pl.ds(0, Q - 1)], recv_sem.at[6])

    wide = jnp.concatenate([recv7[c // per, c % per] for c in range(C)], axis=1)
    term = dot(wide, tokens[...].reshape(wide.shape[1], 128), 1, 0)
    term8[...] = term.astype(bf16)

    def to_plane(i):
        to = far_end(i)

        @pl.when(to != s)
        def _():
            send(term8, recv8.at[s], 7, to, x)

        @pl.when(to == s)
        def _():
            keep(term8, recv8.at[s], 7)

    each(S, to_plane)

    for c in range(C):
        left = jnp.concatenate([disp[c].astype(bf16), recv7[c // per, c % per]], axis=0)
        right = jnp.concatenate([backs[c], params[...]], axis=0)
        gtok[c] = dot(left, right, 0, 0).astype(bf16)
    store_tok = pltpu.make_async_copy(gtok, gtok_h, out_sem.at[2])
    store_tok.start()

    for wait in pending:
        wait()
    store_out.wait()
    store_in.wait()
    store_tok.wait()
    wait_for(recv8, recv_sem.at[7])
    sent(recv8.at[pl.ds(0, S - 1)], 7)


def hand_over(terms_h, a_h, b_h, c_h, to_slot, to_a, to_b, to_c, terms, a, b, c, slot, sem):
    sources, held, targets = (terms_h, a_h, b_h, c_h), (terms, a, b, c), (to_slot, to_a, to_b, to_c)
    ins = [pltpu.make_async_copy(sources[i], held[i], sem.at[i]) for i in range(4)]
    outs = [pltpu.make_async_copy((slot, a, b, c)[i], targets[i], sem.at[4 + i]) for i in range(4)]
    for copy in ins:
        copy.start()
    for i in range(1, 4):
        ins[i].wait()
        outs[i].start()
    ins[0].wait()
    sums = [terms[i].astype(f32) for i in range(4)]
    for i in range(4, terms.shape[0]):
        sums[i % 4] = sums[i % 4] + terms[i].astype(f32)
    slot[...] = (sums[0] + sums[1]) + (sums[2] + sums[3])
    outs[0].start()
    for copy in outs:
        copy.wait()


def solution(mesh):
    S, E = mesh.shape["seq"], mesh.shape["exp"]

    def body(tokens, grad_out, logits, slot_params, weight_in, weight_out):
        C, M, D = tokens.shape
        _, wide, F = weight_in.shape
        args = (tokens, grad_out, logits, slot_params, weight_in[0], weight_out[0])
        outs = (
            jax.ShapeDtypeStruct((C, M, D), bf16),
            jax.ShapeDtypeStruct((E, D), f32),
            jax.ShapeDtypeStruct((wide, F), bf16),
            jax.ShapeDtypeStruct((F, wide), bf16),
        )
        Q = E // 2
        per = C // Q
        hold = lambda a: pltpu.VMEM(a.shape, a.dtype)
        terms = jax.ShapeDtypeStruct((S, E, D), bf16)
        term = jax.ShapeDtypeStruct((E, D), bf16)
        scratch = (
            [hold(a) for a in args]
            + [hold(a) for a in (outs[0], term, outs[2], outs[3])]
            + [
                pltpu.VMEM((C, E, M), f32),
                pltpu.VMEM((C, E, M), f32),
                pltpu.VMEM((E, 16, D), bf16),
                pltpu.VMEM((S, 16, D), bf16),
                pltpu.VMEM((16, D), bf16),
                pltpu.VMEM((E, 16, D), bf16),
                pltpu.VMEM((E, 16, D), bf16),
                pltpu.VMEM((S, 16, D), bf16),
                pltpu.VMEM((16, D), bf16),
                pltpu.VMEM((E, 16, D), bf16),
                pltpu.VMEM((1, 128), f32),
                pltpu.VMEM((S, 128), f32),
                pltpu.VMEM((1, 128), f32),
                pltpu.VMEM((E, 128), f32),
                pltpu.VMEM((128, S), f32),
                pltpu.VMEM((C, E, M), bf16),
                pltpu.VMEM((C // 2, E, M), bf16),
                pltpu.VMEM((Q // 2, per, E, M), bf16),
                pltpu.VMEM((Q, per, E, M), bf16),
                pltpu.VMEM((Q, per, E, M), bf16),
                pltpu.VMEM((8, D), f32),
                pltpu.VMEM((8, D), f32),
                pltpu.SemaphoreType.DMA((6,)),
                pltpu.SemaphoreType.DMA((4,)),
                pltpu.SemaphoreType.DMA((10,)),
                pltpu.SemaphoreType.DMA((10,)),
                pltpu.SemaphoreType.REGULAR,
            ]
        )
        gtok, parts, gwin, gwout = pl.pallas_call(
            functools.partial(kernel, S, E, C),
            out_shape=(outs[0], terms, outs[2], outs[3]),
            in_specs=[pl.BlockSpec(memory_space=pltpu.HBM)] * 6,
            out_specs=[pl.BlockSpec(memory_space=pl.ANY)] * 4,
            scratch_shapes=scratch,
            compiler_params=pltpu.CompilerParams(
                collective_id=0, has_side_effects=True, vmem_limit_bytes=60 << 20
            ),
            name="moe_backward",
        )(*args)
        gslot, gtok, gwin, gwout = pl.pallas_call(
            hand_over,
            out_shape=(outs[1], outs[0], outs[2], outs[3]),
            in_specs=[pl.BlockSpec(memory_space=pl.ANY)] * 4,
            out_specs=[pl.BlockSpec(memory_space=pltpu.HBM)] * 4,
            scratch_shapes=[hold(a) for a in (terms, outs[0], outs[2], outs[3], outs[1])]
            + [pltpu.SemaphoreType.DMA((8,))],
            name="hand_over",
        )(parts, gtok, gwin, gwout)
        return gtok, gslot, gwin[None], gwout[None]

    in_specs = (
        P(None, "seq", "exp"),
        P(None, "seq", "exp"),
        P(None, None, "seq"),
        P(None, "exp"),
        P("exp", None, "seq"),
        P("exp", "seq", None),
    )
    out_specs = (
        P(None, "seq", "exp"),
        P(None, "exp"),
        P("exp", None, "seq"),
        P("exp", "seq", None),
    )
    return jax.shard_map(body, mesh=mesh, in_specs=in_specs, out_specs=out_specs, check_vma=False)
```
